32 devices in a mesh: rep: 8 (over z, x), tp: 4 (over y, core).
Axes of the slice: x: 2, y: 2, z: 4, core: 2. Of those that a mesh axis runs over, the one named last changes fastest.
Arguments:
- x_in: bfloat16 [256, 16384], P('rep', 'tp'), may hold values from -6 to 6
- z_gate: bfloat16 [256, 16384], P('rep', 'tp'), may hold values from -6 to 6
- conv_state: bfloat16 [256, 3, 16384], P('rep', None, 'tp'), may hold values from -6 to 6
- conv_pool: bfloat16 [128, 3, 16384], P('rep', None, 'tp'), may hold values from -6 to 6
- ssm_state: float32 [256, 16, 16384], P('rep', None, 'tp'), may hold values from -6 to 6
- ssm_pool: float32 [128, 16, 16384], P('rep', None, 'tp'), may hold values from -6 to 6
- conv_weight: bfloat16 [4, 16384], P(None, 'tp'), may hold values from -3 to 3
- conv_bias: float32 [16384], P('tp'), may hold values from -0.5 to 0.5
- x_proj: bfloat16 [16384, 544], P('tp'), may hold values from -0.046875 to 0.046875
- dt_gain: float32 [512], replicated, may hold values from 0.5 to 1.5
- b_gain: float32 [16], replicated, may hold values from 0.5 to 1.5
- c_gain: float32 [16], replicated, may hold values from 0.5 to 1.5
- dt_proj: bfloat16 [512, 16384], P(None, 'tp'), may hold values from -0.25 to 0.25
- dt_bias: float32 [16384], P('tp'), may hold values from -3 to 0
- decay_rate: float32 [16, 16384], P(None, 'tp'), may hold values from 0.5 to 16
- skip: float32 [16384], P('tp'), may hold values from 0.5 to 1.5
- query: bfloat16 [256, 8192], P('rep', 'tp'), may hold values from -16 to 16
- new_kv: bfloat16 [256, 2048], P('rep', 'tp'), may hold values from -6 to 6
- kv_cache: bfloat16 [256, 512, 2048], P('rep', None, 'tp'), may hold values from -16 to 16
- kv_pool: bfloat16 [2048, 16, 2048], P('rep', None, 'tp'), may hold values from -16 to 16
- ctx_len: int32 [256], P('rep'), may hold values from 2 to 512
- row_owner: int32 [256], P('rep'), may hold values from -1 to 7, as said below
- row_pos: int32 [256], P('rep'), may hold values from 0 to 1, as said below
- swap_slot: int32 [8, 8, 2], P('rep'), may hold values from 0 to 15, as said below
- swap_lens: int32 [8, 8, 2], P('rep'), may hold values from 2 to 512
- swap_pages: int32 [8, 8, 2, 32], P('rep'), may hold values from 0 to 255
Outputs:
- mamba_out: bfloat16 [256, 16384], P('rep', 'tp')
- attn_out: bfloat16 [256, 8192], P('rep', 'tp')
- new_ssm: float32 [256, 16, 16384], P('rep', None, 'tp')
- new_conv: bfloat16 [256, 3, 16384], P('rep', None, 'tp')
The draws below stay inside these ranges and needn't reach their ends.
Inputs may be any that keep to these rules, and one draw needn't show every extreme that they name: -1 marks a resident request; otherwise the group along rep whose pool holds it. Of one group's rows at most 2 name the same owner, and the pairs (row_owner, row_pos) of one group's resumed rows are distinct; in every draw some group resumes 2 requests from every owner. A resumed request of group g with owner o is entry [o, g, row_pos] of the owner's lists; entries that no request names are unused. `swap_slot`: slots of one owner are distinct. `swap_pages`: only the first ceil(length / 16) pages of a request are read; pages may be shared.
All inputs are finite; a program needn't handle non-finite values.
Results may differ from the reference program's by a relative error of at most 0.013.
Values may be sent and summed in bfloat16 or wider, within the bound.
A program may use at most 128 MiB of HBM per device.

```python
import math
import jax
import jax.numpy as jnp
from jax import lax

E = 16384
N_STATE = 16
DT_RANK = 512
KCONV = 4
HQ = 64
KVH = 8
HD = 128
ROWS = 32
CTX = 512
PAGE = 16
CAP = 2
POOL_PAGES = 256
PAGES = 32
PEERS = 8
SLOTS = 16
SLOTS_ALL = 128
PAGES_ALL = 2048
NREQ = 256
N_REP = 8


def route_counts(key):
    count_key = jax.random.fold_in(key, 101)
    full_key = jax.random.fold_in(key, 102)
    counts = jax.random.randint(count_key, (PEERS, PEERS), 0, CAP + 1)
    full_peer = jax.random.randint(full_key, (), 0, PEERS)
    counts = jnp.where(jnp.arange(PEERS)[None, :] == full_peer, CAP, counts)
    return (counts, full_peer)


def assign_rows(key):
    counts, full_peer = route_counts(key)
    entry_index = jnp.arange(PEERS * CAP)
    entry_owner = entry_index // CAP
    entry_place = entry_index % CAP
    valid = entry_place[None, :] < counts.T[:, entry_owner]
    ranking = jnp.cumsum(valid.astype(jnp.int32), axis=1) - 1
    perm_keys = jax.random.split(jax.random.fold_in(key, 103), PEERS)
    row_perms = jax.vmap(lambda perm_key: jax.random.permutation(perm_key, ROWS))(perm_keys)
    target = jnp.where(valid, jnp.take_along_axis(row_perms, jnp.clip(ranking, 0, ROWS - 1), axis=1), ROWS)
    peer_index = jnp.broadcast_to(jnp.arange(PEERS)[:, None], target.shape)
    owner_values = jnp.broadcast_to(entry_owner[None, :], target.shape).astype(jnp.int32)
    place_values = jnp.broadcast_to(entry_place[None, :], target.shape).astype(jnp.int32)
    owners = jnp.full((PEERS, ROWS), -1, jnp.int32).at[peer_index, target].set(owner_values, mode='drop')
    places = jnp.zeros((PEERS, ROWS), jnp.int32).at[peer_index, target].set(place_values, mode='drop')
    return (owners.reshape(-1), places.reshape(-1))


def draw_row_owner(key, part):
    owners, places = assign_rows(key)
    return owners.astype(jnp.int32)


def draw_row_pos(key, part):
    owners, places = assign_rows(key)
    return places.astype(jnp.int32)


def draw_swap_slot(key, part):
    key = jax.random.fold_in(key, 5)
    slot_keys = jax.random.split(key, PEERS)
    slot_perms = jax.vmap(lambda slot_key: jax.random.permutation(slot_key, SLOTS))(slot_keys)
    return slot_perms.reshape(PEERS, PEERS, CAP).astype(jnp.int32)


def draw_swap_lens(key, part):
    counts, full_peer = route_counts(key)
    key = jax.random.fold_in(key, 3)
    lengths = jax.random.randint(key, (PEERS, PEERS, CAP), 2, CTX + 1)
    owner_pick = jax.random.randint(jax.random.fold_in(key, 4), (), 0, PEERS)
    lengths = lengths.at[owner_pick, full_peer, 0].set(CTX)
    return lengths.astype(jnp.int32)


def draw_ctx_len(key, part):
    key = jax.random.fold_in(key, 6)
    lengths = jax.random.randint(key, (NREQ,), 2, CTX + 1)
    full_rows = jnp.arange(PEERS) * ROWS + jax.random.randint(jax.random.fold_in(key, 7), (PEERS,), 0, ROWS)
    return lengths.at[full_rows].set(CTX).astype(jnp.int32)


def draw_query(key, part):
    key = jax.random.fold_in(key, 8)
    values = jax.random.normal(key, (NREQ, HQ * HD), jnp.float32)
    return values.astype(jnp.bfloat16)


def kv_values(key, count, tokens):
    values = jax.random.normal(key, (count, tokens, KVH, 2, HD), jnp.float32)
    return values.reshape(count, tokens, KVH * 2 * HD).astype(jnp.bfloat16)


def draw_kv_cache(key, part):
    key = jax.random.fold_in(key, 11)
    return kv_values(key, NREQ, CTX)


def draw_kv_pool(key, part):
    key = jax.random.fold_in(key, 12)
    return kv_values(key, PAGES_ALL, PAGE)


def with_ends(values, own_key, smallest, largest):
    longest = values.shape.index(max(values.shape))
    spots = []
    for shift in (0, 1):
        where = [jax.random.randint(jax.random.fold_in(own_key, axis), (), 0, length) for axis, length in enumerate(values.shape)]
        where[longest] = (where[longest] + shift) % values.shape[longest]
        spots.append(tuple(where))
    return values.at[spots[0]].set(smallest).at[spots[1]].set(largest)


def level_of(stream_key, extent, cuts, least, largest):
    def one(axis_at, blocks):
        draws = jax.random.uniform(jax.random.fold_in(jax.random.fold_in(stream_key, 6), axis_at), (blocks,), jnp.float32, least / len(cuts), largest / len(cuts))
        return jnp.repeat(jnp.exp(draws), extent[axis_at] // blocks).reshape((-1,) + (1,) * (len(extent) - axis_at - 1))

    factor_of = one(*cuts[0])
    for cut in cuts[1:]:
        factor_of = factor_of * one(*cut)
    return factor_of


def gaussian(key, extent, width, limit, cuts=(), held_as=jnp.bfloat16):
    values = width * jax.random.normal(key, extent, jnp.float32)
    if cuts:
        values = values * level_of(key, extent, cuts, -0.22, 0.18)
    return jnp.clip(values, -limit, limit).astype(held_as)


def setup_inputs(seed: int = 0) -> dict:
    key_of = jax.random.split(jax.random.key(seed), 27)
    return {
        "x_in": gaussian(key_of[0], (NREQ, E), 1.0, 6.0, ((0, 8), (1, 4))),
        "z_gate": gaussian(key_of[1], (NREQ, E), 1.0, 6.0, ((0, 8), (1, 4))),
        "conv_state": gaussian(key_of[2], (NREQ, KCONV - 1, E), 1.0, 6.0, ((0, 8), (2, 4))),
        "conv_pool": gaussian(key_of[3], (SLOTS_ALL, KCONV - 1, E), 1.0, 6.0, ((0, 8), (2, 4))),
        "ssm_state": gaussian(key_of[4], (NREQ, N_STATE, E), 1.0, 6.0, ((0, 8), (2, 4)), jnp.float32),
        "ssm_pool": gaussian(key_of[5], (SLOTS_ALL, N_STATE, E), 1.0, 6.0, ((0, 8), (2, 4)), jnp.float32),
        "conv_weight": gaussian(key_of[6], (KCONV, E), KCONV ** -0.5, 3.0, ((1, 4),)),
        "conv_bias": jnp.clip(jax.random.uniform(key_of[7], (E,), jnp.float32, -0.5, 0.5) * level_of(key_of[7], (E,), ((0, 4),), -0.4, 0.0), -0.5, 0.5),
        "x_proj": gaussian(key_of[8], (E, DT_RANK + 2 * N_STATE), E ** -0.5, 0.046875, ((0, 4),)),
        "dt_gain": jnp.clip(jax.random.uniform(key_of[9], (DT_RANK,), jnp.float32, 0.5, 1.5), 0.5, 1.5),
        "b_gain": jnp.clip(jax.random.uniform(key_of[10], (N_STATE,), jnp.float32, 0.5, 1.5), 0.5, 1.5),
        "c_gain": jnp.clip(jax.random.uniform(key_of[11], (N_STATE,), jnp.float32, 0.5, 1.5), 0.5, 1.5),
        "dt_proj": gaussian(key_of[12], (DT_RANK, E), DT_RANK ** -0.5, 0.25, ((1, 4),)),
        "dt_bias": jnp.clip(-3.0 + 3.0 * jax.random.uniform(key_of[13], (E,), jnp.float32) ** level_of(key_of[13], (E,), ((0, 4),), -0.2, 0.2), -3.0, 0.0),
        "decay_rate": jnp.clip(jnp.exp(math.log(16.0) - 3.465736 * jax.random.uniform(key_of[14], (N_STATE, E), jnp.float32) ** level_of(key_of[14], (N_STATE, E), ((1, 4),), -0.2, 0.2)), 0.5, 16.0),
        "skip": jnp.clip(0.5 + 1.0 * jax.random.uniform(key_of[15], (E,), jnp.float32) ** level_of(key_of[15], (E,), ((0, 4),), -0.2, 0.2), 0.5, 1.5),
        "query": draw_query(jax.random.fold_in(key_of[26], 71), 0),
        "new_kv": gaussian(key_of[17], (NREQ, 2 * KVH * HD), 1.0, 6.0, ((0, 8), (1, 4))),
        "kv_cache": draw_kv_cache(jax.random.fold_in(key_of[26], 71), 0),
        "kv_pool": draw_kv_pool(jax.random.fold_in(key_of[26], 71), 0),
        "ctx_len": draw_ctx_len(jax.random.fold_in(key_of[26], 71), 0),
        "row_owner": draw_row_owner(jax.random.fold_in(key_of[26], 71), 0),
        "row_pos": draw_row_pos(jax.random.fold_in(key_of[26], 71), 0),
        "swap_slot": draw_swap_slot(jax.random.fold_in(key_of[26], 71), 0),
        "swap_lens": draw_swap_lens(jax.random.fold_in(key_of[26], 71), 0),
        "swap_pages": with_ends(jax.random.randint(key_of[25], (PEERS, PEERS, CAP, PAGES), 0, POOL_PAGES), jax.random.fold_in(key_of[25], 1), 0, POOL_PAGES - 1).astype(jnp.int32),
    }


def attend_block(query_heads, context, ctx_lengths):
    item_count = query_heads.shape[0]
    kv_heads = query_heads.shape[1]
    head_width = query_heads.shape[3]
    kv_pairs = context.astype(jnp.float32).reshape(item_count, context.shape[1], kv_heads, 2, head_width)
    key_rows = kv_pairs[:, :, :, 0, :]
    value_rows = kv_pairs[:, :, :, 1, :]
    score_block = jnp.einsum('nkgd,ntkd->nkgt', query_heads, key_rows) * (1.0 / math.sqrt(head_width))
    live_mask = (jnp.arange(context.shape[1])[None, :] < ctx_lengths[:, None])[:, None, None, :]
    masked = jnp.where(live_mask, score_block, -1e+30)
    score_top = lax.optimization_barrier(jnp.max(masked, axis=-1))
    prob_weights = jnp.where(live_mask, jnp.exp(masked - score_top[..., None]), 0.0).astype(jnp.bfloat16)
    prob_float = prob_weights.astype(jnp.float32)
    prob_total = lax.optimization_barrier(jnp.sum(prob_float, axis=-1))
    attn_mix = jnp.einsum('nkgt,ntkd->nkgd', prob_float, value_rows)
    return (attn_mix, score_top, prob_total)

def finish(query_heads, new_pairs, attn_mix, score_top, prob_total):
    item_count, kv_heads, q_groups, head_width = query_heads.shape
    kv_pairs = new_pairs.astype(jnp.float32).reshape(item_count, kv_heads, 2, head_width)
    new_score = jnp.einsum('nkgd,nkd->nkg', query_heads, kv_pairs[:, :, 0, :]) * (1.0 / math.sqrt(head_width))
    score_peak = jnp.maximum(score_top, new_score)
    old_scale = jnp.exp(score_top - score_peak)
    new_scale = jnp.exp(new_score - score_peak)
    numerator = attn_mix * old_scale[..., None] + new_scale[..., None] * kv_pairs[:, :, None, 1, :]
    result = numerator / (prob_total * old_scale + new_scale)[..., None]
    return result.reshape(item_count, -1).astype(jnp.bfloat16)

def rms_scaled(values, gain):
    return (values * lax.rsqrt(lax.optimization_barrier(jnp.mean(values * values, axis=-1, keepdims=True)) + 1e-06) * gain).astype(jnp.bfloat16)

def reference(x_in, z_gate, conv_state, conv_pool, ssm_state, ssm_pool, conv_weight, conv_bias, x_proj, dt_gain, b_gain, c_gain, dt_proj, dt_bias, decay_rate, skip, query, new_kv, kv_cache, kv_pool, ctx_len, row_owner, row_pos, swap_slot, swap_lens, swap_pages):
    group_count = N_REP

    def by_group(array):
        return array.reshape((group_count, array.shape[0] // group_count) + array.shape[1:])

    def one_group(group_item):
        group, x_rows, z_rows, conv_rows, ssm_rows, query_rows, new_rows, cache_rows, len_rows, owner_rows, pos_rows = group_item
        resumed = owner_rows >= 0
        owner_rank = jnp.maximum(owner_rows, 0).astype(jnp.int32)
        slot_index = (owner_rank * SLOTS + swap_slot[owner_rank, group, pos_rows]).astype(jnp.int32)
        prev_conv = jnp.where(resumed[:, None, None], conv_pool[slot_index], conv_rows)
        prev_ssm = jnp.where(resumed[:, None, None], ssm_pool[slot_index], ssm_rows)
        conv_window = jnp.concatenate([prev_conv, x_rows[:, None, :]], axis=1)
        conv_sum = lax.optimization_barrier(jnp.sum(conv_window.astype(jnp.float32) * conv_weight.astype(jnp.float32)[None], axis=1)) + conv_bias
        mixed_in = jax.nn.silu(conv_sum).astype(jnp.bfloat16)
        proj = jnp.dot(mixed_in, x_proj, preferred_element_type=jnp.float32)
        dt_normed = rms_scaled(proj[:, :DT_RANK], dt_gain)
        dt_step = jax.nn.softplus(jnp.dot(dt_normed, dt_proj, preferred_element_type=jnp.float32) + dt_bias)
        inject = rms_scaled(proj[:, DT_RANK:DT_RANK + N_STATE], b_gain).astype(jnp.float32)
        read_out = rms_scaled(proj[:, DT_RANK + N_STATE:], c_gain).astype(jnp.float32)
        signal = mixed_in.astype(jnp.float32)
        new_state = jnp.exp(-dt_step[:, None, :] * decay_rate[None]) * prev_ssm + (dt_step * signal)[:, None, :] * inject[:, :, None]
        mamba_rows = ((lax.optimization_barrier(jnp.sum(read_out[:, :, None] * new_state, axis=1)) + skip * signal) * jax.nn.silu(z_rows.astype(jnp.float32))).astype(jnp.bfloat16)
        page_index = (owner_rank[:, None] * POOL_PAGES + swap_pages[owner_rank, group, pos_rows]).astype(jnp.int32)
        remote = kv_pool[page_index].reshape(ROWS, CTX, kv_pool.shape[2])
        context = jnp.where(resumed[:, None, None], remote, cache_rows)
        ctx_lengths = jnp.where(resumed, swap_lens[owner_rank, group, pos_rows], len_rows)
        query_heads = query_rows.astype(jnp.float32).reshape(ROWS, KVH, HQ // KVH, HD)
        attn_mix, score_top, prob_total = attend_block(query_heads, context, ctx_lengths)
        attn_rows = finish(query_heads, new_rows, attn_mix, score_top, prob_total)
        return (mamba_rows, attn_rows, new_state, conv_window[:, 1:])
    mamba_all, attn_all, state_all, conv_all = lax.map(one_group, (jnp.arange(group_count).astype(jnp.int32), by_group(x_in), by_group(z_gate), by_group(conv_state), by_group(ssm_state), by_group(query), by_group(new_kv), by_group(kv_cache), by_group(ctx_len), by_group(row_owner), by_group(row_pos)))
    return (mamba_all.reshape(NREQ, E), attn_all.reshape(NREQ, HQ * HD), state_all.reshape(NREQ, N_STATE, E), conv_all.reshape(NREQ, KCONV - 1, E))
```

```python
import functools
import math

import jax
import jax.numpy as jnp
from jax import lax
from jax.experimental import pallas as pl
from jax.experimental.pallas import tpu as pltpu
from jax.sharding import PartitionSpec as P

HD = 128
MESH = pl.DeviceIdType.MESH
VMEM_LIMIT = 48 * 1024 * 1024


def params(**kw):
    return pltpu.CompilerParams(vmem_limit_bytes=VMEM_LIMIT, **kw)


def whole(shape):
    return pl.BlockSpec(shape, lambda *_: (0,) * len(shape))


def attend_row(q, ctx, nkv, length):
    heads, width = q.shape
    kv_heads = nkv.shape[0] // 2
    groups = heads // kv_heads
    tokens = ctx.shape[0]
    scale = 1.0 / math.sqrt(width)

    def of_head(parts):
        row = lax.broadcasted_iota(jnp.int32, parts[0].shape, 0)
        out = parts[0]
        for k in range(1, kv_heads):
            out = jnp.where(row >= k * groups, parts[k], out)
        return out

    nkv = nkv.astype(jnp.float32)
    q32 = q.astype(jnp.float32)
    scores = of_head(
        [
            lax.dot_general(
                q,
                ctx[:, 2 * k * width : (2 * k + 1) * width],
                (((1,), (1,)), ((), ())),
                preferred_element_type=jnp.float32,
            )
            for k in range(kv_heads)
        ]
    ) * scale
    live = lax.broadcasted_iota(jnp.int32, (heads, tokens), 1) < length
    masked = jnp.where(live, scores, -1e30)
    top = jnp.max(masked, axis=1, keepdims=True)
    prob = jnp.where(live, jnp.exp(masked - top), 0.0).astype(jnp.bfloat16)
    total = jnp.sum(prob.astype(jnp.float32), axis=1, keepdims=True)
    mix = of_head(
        [
            jnp.dot(
                prob,
                ctx[:, (2 * k + 1) * width : (2 * k + 2) * width],
                preferred_element_type=jnp.float32,
            )
            for k in range(kv_heads)
        ]
    )
    new_key = of_head(
        [jnp.broadcast_to(nkv[2 * k : 2 * k + 1], (heads, width)) for k in range(kv_heads)]
    )
    new_value = of_head(
        [jnp.broadcast_to(nkv[2 * k + 1 : 2 * k + 2], (heads, width)) for k in range(kv_heads)]
    )
    new_score = jnp.sum(q32 * new_key, axis=1, keepdims=True) * scale
    peak = jnp.maximum(top, new_score)
    old_scale = jnp.exp(top - peak)
    new_scale = jnp.exp(new_score - peak)
    result = (mix * old_scale + new_scale * new_value) / (total * old_scale + new_scale)
    return result.astype(jnp.bfloat16)


def resident_kernel(lens, q_ref, kv_ref, nkv_ref, out_ref):
    batch = q_ref.shape[0]
    base = pl.program_id(0) * batch
    rows = [attend_row(q_ref[i], kv_ref[i], nkv_ref[i], lens[base + i]) for i in range(batch)]
    for i in range(batch):
        out_ref[i] = rows[i]


def paged_kernel(lens, pages, q_ref, pool_ref, nkv_ref, out_ref, ctx_ref):
    batch = q_ref.shape[0]
    base = pl.program_id(0) * batch
    page = pool_ref.shape[1]
    page_count = ctx_ref.shape[1] // page
    for i in range(batch):
        for j in range(page_count):
            ctx_ref[i, j * page : (j + 1) * page, :] = pool_ref[pages[(base + i) * page_count + j]]
    rows = [attend_row(q_ref[i], ctx_ref[i], nkv_ref[i], lens[base + i]) for i in range(batch)]
    for i in range(batch):
        out_ref[i] = rows[i]


def attend_resident(q, kv, nkv, lens):
    rows, heads, width = q.shape
    tokens, kv_width = kv.shape[1:]
    batch = 4
    return pl.pallas_call(
        resident_kernel,
        grid_spec=pltpu.PrefetchScalarGridSpec(
            num_scalar_prefetch=1,
            grid=(rows // batch,),
            in_specs=[
                pl.BlockSpec((batch, heads, width), lambda i, *_: (i, 0, 0)),
                pl.BlockSpec((batch, tokens, kv_width), lambda i, *_: (i, 0, 0)),
                pl.BlockSpec((batch,) + nkv.shape[1:], lambda i, *_: (i, 0, 0)),
            ],
            out_specs=pl.BlockSpec((batch, heads, width), lambda i, *_: (i, 0, 0)),
        ),
        out_shape=jax.ShapeDtypeStruct(q.shape, jnp.bfloat16),
        compiler_params=params(),
        cost_estimate=pl.CostEstimate(
            flops=rows * tokens * heads * width * 8,
            bytes_accessed=2 * kv.size,
            transcendentals=rows * heads * tokens,
        ),
        name="attend_resident",
    )(lens, q, kv, nkv)


def attend_paged(q, pool, nkv, lens, pages, tokens):
    entries, heads, width = q.shape
    batch = 4
    return pl.pallas_call(
        paged_kernel,
        grid_spec=pltpu.PrefetchScalarGridSpec(
            num_scalar_prefetch=2,
            grid=(entries // batch,),
            in_specs=[
                pl.BlockSpec((batch, heads, width), lambda i, *_: (i, 0, 0)),
                whole(pool.shape),
                pl.BlockSpec((batch,) + nkv.shape[1:], lambda i, *_: (i, 0, 0)),
            ],
            out_specs=pl.BlockSpec((batch, heads, width), lambda i, *_: (i, 0, 0)),
            scratch_shapes=[pltpu.VMEM((batch, tokens, pool.shape[2]), jnp.bfloat16)],
        ),
        out_shape=jax.ShapeDtypeStruct(q.shape, jnp.bfloat16),
        compiler_params=params(),
        cost_estimate=pl.CostEstimate(
            flops=entries * tokens * heads * width * 8,
            bytes_accessed=2 * pool.size,
            transcendentals=entries * heads * tokens,
        ),
        name="attend_paged",
    )(lens, pages, q, pool, nkv)


def pack_kernel(slots, pool_ref, out_ref):
    out_ref[...] = pool_ref[...].astype(jnp.bfloat16)


def pack_states(pool, slots):
    entries = slots.shape[0]
    block = (1,) + pool.shape[1:]
    return pl.pallas_call(
        pack_kernel,
        grid_spec=pltpu.PrefetchScalarGridSpec(
            num_scalar_prefetch=1,
            grid=(entries,),
            in_specs=[pl.BlockSpec(block, lambda i, slots: (slots[i], 0, 0))],
            out_specs=pl.BlockSpec(block, lambda i, slots: (i, 0, 0)),
        ),
        out_shape=jax.ShapeDtypeStruct((entries,) + pool.shape[1:], jnp.bfloat16),
        compiler_params=params(),
        cost_estimate=pl.CostEstimate(
            flops=0, bytes_accessed=6 * entries * pool[0].size, transcendentals=0
        ),
        name="pack_states",
    )(slots, pool)


def conv_kernel(source, x_ref, state_ref, got_ref, weight_ref, bias_ref, proj_ref,
                mixed_ref, conv_ref, part_ref, sum_ref):
    rows, taps = state_ref.shape[:2]
    weight = weight_ref[...].astype(jnp.float32)
    for r in range(rows):
        entry = source[r]
        prev = jnp.where(
            entry >= 0,
            got_ref[jnp.maximum(entry, 0)].astype(jnp.float32)[:taps],
            state_ref[r].astype(jnp.float32),
        )
        new = x_ref[r : r + 1, :].astype(jnp.float32)
        conv_ref[r] = jnp.concatenate([prev[1:], new], axis=0).astype(jnp.bfloat16)
        sum_ref[r : r + 1, :] = (
            jnp.sum(prev * weight[:taps], axis=0, keepdims=True) + new * weight[taps:]
        )
    total = sum_ref[...] + bias_ref[...]
    mixed = (total / (1.0 + jnp.exp(-total))).astype(jnp.bfloat16)
    mixed_ref[...] = mixed.astype(jnp.float32)
    part_ref[...] = jnp.dot(mixed, proj_ref[...], preferred_element_type=jnp.float32)


def convolve(source, x_in, state, got, weight, bias, x_proj):
    rows, channels = x_in.shape
    outs = (
        jax.ShapeDtypeStruct((rows, channels), jnp.float32),
        jax.ShapeDtypeStruct(state.shape, jnp.bfloat16),
        jax.ShapeDtypeStruct((rows, x_proj.shape[1]), jnp.float32),
    )
    operands = (x_in, state, got, weight, bias, x_proj)
    return pl.pallas_call(
        conv_kernel,
        grid_spec=pltpu.PrefetchScalarGridSpec(
            num_scalar_prefetch=1,
            grid=(1,),
            in_specs=[whole(a.shape) for a in operands],
            out_specs=[whole(o.shape) for o in outs],
            scratch_shapes=[pltpu.VMEM((rows, channels), jnp.float32)],
        ),
        out_shape=outs,
        compiler_params=params(),
        cost_estimate=pl.CostEstimate(
            flops=2 * rows * x_proj.size, bytes_accessed=2 * x_proj.size + 8 * x_in.size * 2,
            transcendentals=x_in.size,
        ),
        name="conv_proj",
    )(source, *operands)


def step_kernel(count, part_ref, dt_proj_ref, bias_ref, dt_gain_ref, b_gain_ref, c_gain_ref,
                dt_ref, bc_ref, got_ref, send_sem, recv_sem):
    me = lax.axis_index("tp")
    barrier = pltpu.get_barrier_semaphore()
    for k in range(1, count):
        pl.semaphore_signal(
            barrier, inc=1, device_id={"tp": lax.rem(me + k, count)}, device_id_type=MESH
        )
    pl.semaphore_wait(barrier, count - 1)
    copies = []
    for k in range(1, count):
        copy = pltpu.make_async_remote_copy(
            src_ref=part_ref,
            dst_ref=got_ref.at[k - 1],
            send_sem=send_sem.at[k - 1],
            recv_sem=recv_sem.at[k - 1],
            device_id={"tp": lax.rem(me + k, count)},
            device_id_type=MESH,
        )
        copy.start()
        copies.append(copy)
    proj = part_ref[...]
    for k, copy in enumerate(copies):
        copy.wait_recv()
        proj = proj + got_ref[k]
    rank = dt_proj_ref.shape[0]
    states = b_gain_ref.shape[1]

    def rms_scaled(values, gain):
        mean = jnp.mean(values * values, axis=-1, keepdims=True)
        return (values * lax.rsqrt(mean + 1e-06) * gain).astype(jnp.bfloat16)

    normed = rms_scaled(proj[:, :rank], dt_gain_ref[...])
    raw = jnp.dot(normed, dt_proj_ref[...], preferred_element_type=jnp.float32) + bias_ref[...]
    dt_ref[...] = jnp.maximum(raw, 0.0) + jnp.log1p(jnp.exp(-jnp.abs(raw)))
    bc_ref[0] = rms_scaled(proj[:, rank : rank + states], b_gain_ref[...]).astype(jnp.float32)
    bc_ref[1] = rms_scaled(proj[:, rank + states :], c_gain_ref[...]).astype(jnp.float32)
    for copy in copies:
        copy.wait_send()


def step_sizes(count, part, dt_proj, dt_bias, dt_gain, b_gain, c_gain):
    rows = part.shape[0]
    channels = dt_proj.shape[1]
    vmem = pl.BlockSpec(memory_space=pltpu.VMEM)
    return pl.pallas_call(
        functools.partial(step_kernel, count),
        out_shape=(
            jax.ShapeDtypeStruct((rows, channels), jnp.float32),
            jax.ShapeDtypeStruct((2, rows, b_gain.shape[1]), jnp.float32),
        ),
        in_specs=[vmem] * 6,
        out_specs=(vmem, vmem),
        scratch_shapes=[
            pltpu.VMEM((count - 1,) + part.shape, jnp.float32),
            pltpu.SemaphoreType.DMA((count - 1,)),
            pltpu.SemaphoreType.DMA((count - 1,)),
        ],
        compiler_params=params(collective_id=0, has_side_effects=True),
        cost_estimate=pl.CostEstimate(
            flops=2 * rows * dt_proj.size, bytes_accessed=2 * dt_proj.size + 4 * rows * channels,
            transcendentals=2 * rows * channels,
        ),
        name="tp_sum_step",
    )(part, dt_proj, dt_bias, dt_gain, b_gain, c_gain)


def update_row(row, prev, dt_ref, signal_ref, bc_ref, decay_ref):
    states = decay_ref.shape[0]
    eye = lax.broadcasted_iota(jnp.int32, (states, states), 0) == lax.broadcasted_iota(
        jnp.int32, (states, states), 1
    )

    def column(which):
        line = bc_ref[which, pl.ds(row, 1), :]
        spread = jnp.where(eye, jnp.broadcast_to(line, (states, states)), 0.0)
        return jnp.sum(spread, axis=1, keepdims=True)

    dt = dt_ref[pl.ds(row, 1), :]
    drive = dt * signal_ref[pl.ds(row, 1), :]
    new = jnp.exp(-dt * decay_ref[...]) * prev + drive * column(0)
    return new, jnp.sum(column(1) * new, axis=0, keepdims=True)


def early_kernel(perm, state_ref, dt_ref, signal_ref, bc_ref, decay_ref, new_ref, y_ref, *, first):
    step = pl.program_id(0)

    @pl.when(step == 0)
    def _():
        y_ref[...] = jnp.zeros_like(y_ref)

    row = perm[first + step]
    new, y = update_row(row, state_ref[0], dt_ref, signal_ref, bc_ref, decay_ref)
    new_ref[0] = new
    y_ref[pl.ds(row, 1), :] = y


def late_kernel(perm, source, state_ref, got_ref, dt_ref, signal_ref, bc_ref, decay_ref, early_y,
                skip_ref, z_ref, kept_ref, new_ref, out_ref, y_ref):
    step = pl.program_id(0)

    @pl.when(step == 0)
    def _():
        y_ref[...] = early_y[...]

    row = perm[step]
    prev = jnp.where(source[row] >= 0, got_ref[0].astype(jnp.float32), state_ref[0])
    new, y = update_row(row, prev, dt_ref, signal_ref, bc_ref, decay_ref)
    new_ref[0] = new
    y_ref[pl.ds(row, 1), :] = y

    @pl.when(step == pl.num_programs(0) - 1)
    def _():
        z = z_ref[...].astype(jnp.float32)
        gate = z / (1.0 + jnp.exp(-z))
        out_ref[...] = ((y_ref[...] + skip_ref[...] * signal_ref[...]) * gate).astype(jnp.bfloat16)


def update_early(perm, state, dt, signal, bc, decay, late):
    rows = state.shape[0]
    block = (1,) + state.shape[1:]
    shared = (dt, signal, bc, decay)
    return pl.pallas_call(
        functools.partial(early_kernel, first=late),
        grid_spec=pltpu.PrefetchScalarGridSpec(
            num_scalar_prefetch=1,
            grid=(rows - late,),
            in_specs=[pl.BlockSpec(block, lambda i, perm: (perm[late + i], 0, 0))]
            + [whole(a.shape) for a in shared],
            out_specs=[
                pl.BlockSpec(block, lambda i, perm: (perm[late + i], 0, 0)),
                whole(dt.shape),
            ],
        ),
        out_shape=(
            jax.ShapeDtypeStruct(state.shape, jnp.float32),
            jax.ShapeDtypeStruct(dt.shape, jnp.float32),
        ),
        compiler_params=params(),
        cost_estimate=pl.CostEstimate(
            flops=8 * (rows - late) * state[0].size,
            bytes_accessed=8 * (rows - late) * state[0].size,
            transcendentals=(rows - late) * state[0].size,
        ),
        name="ssm_early",
    )(perm, state, *shared)


def update_late(perm, source, state, got, dt, signal, bc, decay, early_y, skip, z, kept, late):
    block = (1,) + state.shape[1:]
    shared = (dt, signal, bc, decay, early_y, skip, z)
    return pl.pallas_call(
        late_kernel,
        grid_spec=pltpu.PrefetchScalarGridSpec(
            num_scalar_prefetch=2,
            grid=(late,),
            in_specs=[
                pl.BlockSpec(block, lambda i, perm, source: (perm[i], 0, 0)),
                pl.BlockSpec(
                    block, lambda i, perm, source: (jnp.maximum(source[perm[i]], 0), 0, 0)
                ),
            ]
            + [whole(a.shape) for a in shared]
            + [pl.BlockSpec(memory_space=pl.ANY)],
            out_specs=[
                pl.BlockSpec(block, lambda i, perm, source: (perm[i], 0, 0)),
                whole(dt.shape),
            ],
            scratch_shapes=[pltpu.VMEM(dt.shape, jnp.float32)],
        ),
        out_shape=(
            jax.ShapeDtypeStruct(state.shape, jnp.float32),
            jax.ShapeDtypeStruct(dt.shape, jnp.bfloat16),
        ),
        input_output_aliases={4 + len(shared): 0},
        compiler_params=params(),
        cost_estimate=pl.CostEstimate(
            flops=8 * late * state[0].size,
            bytes_accessed=10 * late * state[0].size,
            transcendentals=late * state[0].size,
        ),
        name="ssm_late",
    )(perm, source, state, got, *shared, kept)


def shards(
    x_in,
    z_gate,
    conv_state,
    conv_pool,
    ssm_state,
    ssm_pool,
    conv_weight,
    conv_bias,
    x_proj,
    dt_gain,
    b_gain,
    c_gain,
    dt_proj,
    dt_bias,
    decay_rate,
    skip,
    query,
    new_kv,
    kv_cache,
    kv_pool,
    ctx_len,
    row_owner,
    row_pos,
    swap_slot,
    swap_lens,
    swap_pages,
):
    peer_count = lax.axis_size("rep")
    tp_count = lax.axis_size("tp")
    row_count, channels = x_in.shape
    slot_cap = swap_slot.shape[2]
    entry_count = peer_count * slot_cap
    taps = conv_state.shape[1]
    head_count = query.shape[1] // HD
    slot_list = swap_slot[0].reshape(-1)
    resumed = row_owner >= 0
    source = jnp.where(resumed, row_owner * slot_cap + row_pos, -1).astype(jnp.int32)
    row_ids = jnp.arange(row_count, dtype=jnp.int32)
    entry_ids = jnp.arange(entry_count, dtype=jnp.int32)
    match = source[None, :] == entry_ids[:, None]
    entry_row = jnp.sum(jnp.where(match, row_ids[None, :], 0), axis=1)
    before = row_ids[None, :] < row_ids[:, None]
    earlier = jnp.sum((before & (resumed[None, :] == resumed[:, None])).astype(jnp.int32), axis=1)
    place = jnp.where(resumed, earlier, earlier + jnp.sum(resumed.astype(jnp.int32)))
    perm = jnp.sum(
        jnp.where(place[None, :] == row_ids[:, None], row_ids[None, :], 0), axis=1
    ).astype(jnp.int32)

    def exchange(block):
        split = block.reshape((peer_count, slot_cap) + block.shape[1:])
        out = lax.all_to_all(split, "rep", split_axis=0, concat_axis=0, tiled=True)
        return out.reshape(block.shape)

    asked = jnp.take(jnp.concatenate([query, new_kv], axis=1), entry_row, axis=0, mode="clip")
    asked = jnp.pad(asked, ((0, 0), (0, channels - asked.shape[1])))
    taps_out = jnp.take(conv_pool, slot_list, axis=0, mode="clip")
    first = exchange(jnp.concatenate([taps_out, asked[:, None, :]], axis=1))

    states = pack_states(ssm_pool, slot_list)
    first, states = lax.optimization_barrier((first, states))
    states_in = exchange(states)

    query_rows = query.reshape(row_count, head_count, HD)
    new_rows = new_kv.reshape(row_count, -1, HD)
    attn_here = attend_resident(query_rows, kv_cache, new_rows, ctx_len).reshape(query.shape)

    mixed, new_conv, part = convolve(
        source, x_in, conv_state, first, conv_weight, conv_bias[None, :], x_proj
    )
    dt_step, bc = step_sizes(
        tp_count, part, dt_proj, dt_bias[None, :], dt_gain[None, :], b_gain[None, :],
        c_gain[None, :],
    )

    query_width = query.shape[1]
    asked_in = first[:, taps, :]
    query_in = asked_in[:, :query_width].reshape(entry_count, head_count, HD)
    new_in = asked_in[:, query_width : query_width + new_kv.shape[1]].reshape(entry_count, -1, HD)
    attn_there = attend_paged(
        query_in, kv_pool, new_in, swap_lens[0].reshape(-1), swap_pages[0].reshape(-1),
        kv_cache.shape[1],
    ).reshape(entry_count, query_width)
    attn_back = exchange(attn_there)
    picked = jnp.take(attn_back, jnp.maximum(source, 0), axis=0, mode="clip")
    attn_out = jnp.where(resumed[:, None], picked, attn_here)

    late = min(row_count, entry_count)
    if late < row_count:
        kept, early_y = update_early(perm, ssm_state, dt_step, mixed, bc, decay_rate, late)
    else:
        kept, early_y = jnp.zeros_like(ssm_state), jnp.zeros_like(dt_step)
    new_ssm, mamba_out = update_late(
        perm, source, ssm_state, states_in, dt_step, mixed, bc, decay_rate, early_y,
        skip[None, :], z_gate, kept, late,
    )
    return (mamba_out, attn_out, new_ssm, new_conv)


def solution(mesh):
    in_specs = (
        P("rep", "tp"),
        P("rep", "tp"),
        P("rep", None, "tp"),
        P("rep", None, "tp"),
        P("rep", None, "tp"),
        P("rep", None, "tp"),
        P(None, "tp"),
        P("tp"),
        P("tp", None),
        P(),
        P(),
        P(),
        P(None, "tp"),
        P("tp"),
        P(None, "tp"),
        P("tp"),
        P("rep", "tp"),
        P("rep", "tp"),
        P("rep", None, "tp"),
        P("rep", None, "tp"),
        P("rep"),
        P("rep"),
        P("rep"),
        P("rep", None, None),
        P("rep", None, None),
        P("rep", None, None, None),
    )
    out_specs = (P("rep", "tp"), P("rep", "tp"), P("rep", None, "tp"), P("rep", None, "tp"))
    return jax.shard_map(shards, mesh=mesh, in_specs=in_specs, out_specs=out_specs, check_vma=False)
```

```python
import functools
import math

import jax
import jax.numpy as jnp
from jax import lax
from jax.experimental import pallas as pl
from jax.experimental.pallas import tpu as pltpu
from jax.sharding import PartitionSpec as P

HD = 128
MESH = pl.DeviceIdType.MESH
BATCH = 4
VMEM_LIMIT = 48 * 1024 * 1024


def params(**kw):
    return pltpu.CompilerParams(vmem_limit_bytes=VMEM_LIMIT, **kw)


def whole(shape):
    return pl.BlockSpec(shape, lambda *_: (0,) * len(shape))


def attend_row(q, ctx, nkv, length):
    heads, width = q.shape
    kv_heads = nkv.shape[0] // 2
    groups = heads // kv_heads
    tokens = ctx.shape[0]
    scale = 1.0 / math.sqrt(width)

    def of_head(parts):
        row = lax.broadcasted_iota(jnp.int32, parts[0].shape, 0)
        out = parts[0]
        for k in range(1, kv_heads):
            out = jnp.where(row >= k * groups, parts[k], out)
        return out

    nkv = nkv.astype(jnp.float32)
    q32 = q.astype(jnp.float32)
    scores = of_head(
        [
            lax.dot_general(
                q,
                ctx[:, 2 * k * width : (2 * k + 1) * width],
                (((1,), (1,)), ((), ())),
                preferred_element_type=jnp.float32,
            )
            for k in range(kv_heads)
        ]
    ) * scale
    live = lax.broadcasted_iota(jnp.int32, (heads, tokens), 1) < length
    masked = jnp.where(live, scores, -1e30)
    top = jnp.max(masked, axis=1, keepdims=True)
    prob = jnp.where(live, jnp.exp(masked - top), 0.0).astype(jnp.bfloat16)
    total = jnp.sum(prob.astype(jnp.float32), axis=1, keepdims=True)
    mix = of_head(
        [
            jnp.dot(
                prob,
                ctx[:, (2 * k + 1) * width : (2 * k + 2) * width],
                preferred_element_type=jnp.float32,
            )
            for k in range(kv_heads)
        ]
    )
    new_key = of_head(
        [jnp.broadcast_to(nkv[2 * k : 2 * k + 1], (heads, width)) for k in range(kv_heads)]
    )
    new_value = of_head(
        [jnp.broadcast_to(nkv[2 * k + 1 : 2 * k + 2], (heads, width)) for k in range(kv_heads)]
    )
    new_score = jnp.sum(q32 * new_key, axis=1, keepdims=True) * scale
    peak = jnp.maximum(top, new_score)
    old_scale = jnp.exp(top - peak)
    new_scale = jnp.exp(new_score - peak)
    result = (mix * old_scale + new_scale * new_value) / (total * old_scale + new_scale)
    return result.astype(jnp.bfloat16)


def resident_kernel(lens, q_ref, kv_ref, nkv_ref, out_ref):
    batch = q_ref.shape[0]
    base = pl.program_id(0) * batch
    rows = [attend_row(q_ref[i], kv_ref[i], nkv_ref[i], lens[base + i]) for i in range(batch)]
    for i in range(batch):
        out_ref[i] = rows[i]


def paged_kernel(lens, pages, q_ref, pool_ref, nkv_ref, out_ref, ctx_ref):
    batch = q_ref.shape[0]
    base = pl.program_id(0) * batch
    page = pool_ref.shape[1]
    page_count = ctx_ref.shape[1] // page
    for i in range(batch):
        for j in range(page_count):
            ctx_ref[i, j * page : (j + 1) * page, :] = pool_ref[pages[(base + i) * page_count + j]]
    rows = [attend_row(q_ref[i], ctx_ref[i], nkv_ref[i], lens[base + i]) for i in range(batch)]
    for i in range(batch):
        out_ref[i] = rows[i]


def attend_resident(q, kv, nkv, lens):
    rows, heads, width = q.shape
    tokens, kv_width = kv.shape[1:]
    batch = BATCH
    return pl.pallas_call(
        resident_kernel,
        grid_spec=pltpu.PrefetchScalarGridSpec(
            num_scalar_prefetch=1,
            grid=(rows // batch,),
            in_specs=[
                pl.BlockSpec((batch, heads, width), lambda i, *_: (i, 0, 0)),
                pl.BlockSpec((batch, tokens, kv_width), lambda i, *_: (i, 0, 0)),
                pl.BlockSpec((batch,) + nkv.shape[1:], lambda i, *_: (i, 0, 0)),
            ],
            out_specs=pl.BlockSpec((batch, heads, width), lambda i, *_: (i, 0, 0)),
        ),
        out_shape=jax.ShapeDtypeStruct(q.shape, jnp.bfloat16),
        compiler_params=params(),
        cost_estimate=pl.CostEstimate(
            flops=rows * tokens * heads * width * 8,
            bytes_accessed=2 * kv.size,
            transcendentals=rows * heads * tokens,
        ),
        name="attend_resident",
    )(lens, q, kv, nkv)


def attend_paged(q, pool, nkv, lens, pages, tokens):
    entries, heads, width = q.shape
    batch = BATCH
    return pl.pallas_call(
        paged_kernel,
        grid_spec=pltpu.PrefetchScalarGridSpec(
            num_scalar_prefetch=2,
            grid=(entries // batch,),
            in_specs=[
                pl.BlockSpec((batch, heads, width), lambda i, *_: (i, 0, 0)),
                whole(pool.shape),
                pl.BlockSpec((batch,) + nkv.shape[1:], lambda i, *_: (i, 0, 0)),
            ],
            out_specs=pl.BlockSpec((batch, heads, width), lambda i, *_: (i, 0, 0)),
            scratch_shapes=[pltpu.VMEM((batch, tokens, pool.shape[2]), jnp.bfloat16)],
        ),
        out_shape=jax.ShapeDtypeStruct(q.shape, jnp.bfloat16),
        compiler_params=params(),
        cost_estimate=pl.CostEstimate(
            flops=entries * tokens * heads * width * 8,
            bytes_accessed=2 * pool.size,
            transcendentals=entries * heads * tokens,
        ),
        name="attend_paged",
    )(lens, pages, q, pool, nkv)


def pack_kernel(slots, *refs):
    out_ref = refs[-1]
    for k, ref in enumerate(refs[:-1]):
        out_ref[k] = ref[0].astype(jnp.bfloat16)


def pack_states(pool, slots):
    entries = slots.shape[0]
    block = (1,) + pool.shape[1:]

    def spec(k):
        return pl.BlockSpec(block, lambda i, slots: (slots[i * BATCH + k], 0, 0))

    return pl.pallas_call(
        pack_kernel,
        grid_spec=pltpu.PrefetchScalarGridSpec(
            num_scalar_prefetch=1,
            grid=(entries // BATCH,),
            in_specs=[spec(k) for k in range(BATCH)],
            out_specs=pl.BlockSpec((BATCH,) + pool.shape[1:], lambda i, slots: (i, 0, 0)),
        ),
        out_shape=jax.ShapeDtypeStruct((entries,) + pool.shape[1:], jnp.bfloat16),
        compiler_params=params(),
        cost_estimate=pl.CostEstimate(
            flops=0, bytes_accessed=6 * entries * pool[0].size, transcendentals=0
        ),
        name="pack_states",
    )(slots, *([pool] * BATCH))


def entry_match(owner_ref, pos_ref, entries, cap):
    owner = owner_ref[...]
    source = jnp.where(owner >= 0, owner * cap + pos_ref[...], -1)
    shape = (entries, owner.shape[1])
    hit = lax.broadcasted_iota(jnp.int32, shape, 0) == jnp.broadcast_to(source, shape)
    return jnp.where(hit, 1.0, 0.0).astype(jnp.bfloat16)


def pick(match, rows, contract):
    return lax.dot_general(
        match, rows, (((contract,), (0,)), ((), ())), preferred_element_type=jnp.float32
    )


def ask_kernel(cap, owner_ref, pos_ref, slot_ref, pool_ref, query_ref, new_ref, out_ref):
    taps, slots, channels = pool_ref.shape
    entries = out_ref.shape[0]
    shape = (slots, entries)
    hit = lax.broadcasted_iota(jnp.int32, shape, 0) == jnp.broadcast_to(slot_ref[...], shape)
    chosen = jnp.where(hit, 1.0, 0.0).astype(jnp.bfloat16)
    for j in range(taps):
        out_ref[:, j * channels : (j + 1) * channels] = pick(chosen, pool_ref[j], 0).astype(
            jnp.bfloat16
        )
    match = entry_match(owner_ref, pos_ref, entries, cap)
    at = taps * channels
    for ref in (query_ref, new_ref):
        out_ref[:, at : at + ref.shape[1]] = pick(match, ref[...], 1).astype(jnp.bfloat16)
        at += ref.shape[1]


def ask(cap, owner, pos, slots, pool, query, new_kv):
    entries = slots.shape[1]
    operands = (owner, pos, slots, pool, query, new_kv)
    width = pool.shape[0] * pool.shape[2] + query.shape[1] + new_kv.shape[1]
    return pl.pallas_call(
        functools.partial(ask_kernel, cap),
        grid=(1,),
        in_specs=[whole(a.shape) for a in operands],
        out_specs=whole((entries, width)),
        out_shape=jax.ShapeDtypeStruct((entries, width), jnp.bfloat16),
        compiler_params=params(),
        cost_estimate=pl.CostEstimate(
            flops=2 * entries * pool.size, bytes_accessed=4 * pool.size, transcendentals=0
        ),
        name="ask",
    )(*operands)


def conv_kernel(cap, owner_ref, pos_ref, x_ref, state_ref, got_ref, weight_ref, bias_ref,
                proj_ref, mixed_ref, conv_ref, part_ref):
    taps, rows, channels = state_ref.shape
    entries = got_ref.shape[0]
    match = entry_match(owner_ref, pos_ref, entries, cap)
    resumed = pick(match, jnp.ones((entries, 128), jnp.bfloat16), 0)[:, :1] > 0.5
    new = x_ref[...]
    total = new.astype(jnp.float32) * weight_ref[taps : taps + 1, :].astype(jnp.float32)
    for j in range(taps):
        theirs = pick(match, got_ref[:, j * channels : (j + 1) * channels], 0)
        prev = jnp.where(resumed, theirs, state_ref[j].astype(jnp.float32))
        if j > 0:
            conv_ref[j - 1] = prev.astype(jnp.bfloat16)
        total = total + prev * weight_ref[j : j + 1, :].astype(jnp.float32)
    conv_ref[taps - 1] = new
    total = total + bias_ref[...]
    mixed = (total / (1.0 + jnp.exp(-total))).astype(jnp.bfloat16)
    mixed_ref[...] = mixed.astype(jnp.float32)
    part_ref[...] = lax.dot_general(
        mixed, proj_ref[...], (((1,), (1,)), ((), ())), preferred_element_type=jnp.float32
    )


def convolve(cap, owner, pos, x_in, state, got, weight, bias, proj):
    rows, channels = x_in.shape
    outs = (
        jax.ShapeDtypeStruct((rows, channels), jnp.float32),
        jax.ShapeDtypeStruct(state.shape, jnp.bfloat16),
        jax.ShapeDtypeStruct((rows, proj.shape[0]), jnp.float32),
    )
    operands = (owner, pos, x_in, state, got, weight, bias, proj)
    return pl.pallas_call(
        functools.partial(conv_kernel, cap),
        grid=(1,),
        in_specs=[whole(a.shape) for a in operands],
        out_specs=[whole(o.shape) for o in outs],
        out_shape=outs,
        compiler_params=params(),
        cost_estimate=pl.CostEstimate(
            flops=2 * rows * proj.size, bytes_accessed=2 * proj.size + 16 * x_in.size,
            transcendentals=x_in.size,
        ),
        name="conv_proj",
    )(*operands)


def step_kernel(count, peers, part_ref, attn_ref, dt_proj_ref, bias_ref, dt_gain_ref, b_gain_ref,
                c_gain_ref, dt_ref, bc_ref, back_ref, got_ref, home_ref, send_sem, recv_sem,
                home_send, home_recv):
    me = lax.axis_index("tp")
    group = lax.axis_index("rep")
    barrier = pltpu.get_barrier_semaphore()
    partners = [{"tp": lax.rem(me + k, count)} for k in range(1, count)]
    homes = [lax.rem(group + k, peers) for k in range(1, peers)]
    for partner in partners + [{"rep": home} for home in homes]:
        pl.semaphore_signal(barrier, inc=1, device_id=partner, device_id_type=MESH)
    pl.semaphore_wait(barrier, count + peers - 2)
    copies = []
    for k, partner in enumerate(partners):
        copy = pltpu.make_async_remote_copy(
            src_ref=part_ref,
            dst_ref=got_ref.at[k],
            send_sem=send_sem.at[k],
            recv_sem=recv_sem.at[k],
            device_id=partner,
            device_id_type=MESH,
        )
        copy.start()
        copies.append(copy)
    returns = []
    for k, home in enumerate(homes):
        copy = pltpu.make_async_remote_copy(
            src_ref=attn_ref.at[home],
            dst_ref=home_ref.at[k],
            send_sem=home_send.at[k],
            recv_sem=home_recv.at[k],
            device_id={"rep": home},
            device_id_type=MESH,
        )
        copy.start()
        returns.append(copy)
    proj = part_ref[...]
    for k, copy in enumerate(copies):
        copy.wait_recv()
        proj = proj + got_ref[k]
    rank = dt_proj_ref.shape[0]
    states = b_gain_ref.shape[1]

    def rms_scaled(values, gain):
        mean = jnp.mean(values * values, axis=-1, keepdims=True)
        return (values * lax.rsqrt(mean + 1e-06) * gain).astype(jnp.bfloat16)

    normed = rms_scaled(proj[:, :rank], dt_gain_ref[...])
    raw = jnp.dot(normed, dt_proj_ref[...], preferred_element_type=jnp.float32) + bias_ref[...]
    dt_ref[...] = jnp.maximum(raw, 0.0) + jnp.log1p(jnp.exp(-jnp.abs(raw)))
    bc_ref[0] = rms_scaled(proj[:, rank : rank + states], b_gain_ref[...]).astype(jnp.float32)
    bc_ref[1] = rms_scaled(proj[:, rank + states :], c_gain_ref[...]).astype(jnp.float32)
    back_ref[group] = attn_ref[group]
    for k, copy in enumerate(returns):
        copy.wait_recv()
        back_ref[lax.rem(group + peers - 1 - k, peers)] = home_ref[k]
    for copy in copies + returns:
        copy.wait_send()


def step_sizes(count, part, attn, dt_proj, dt_bias, dt_gain, b_gain, c_gain):
    rows = part.shape[0]
    peers = attn.shape[0]
    channels = dt_proj.shape[1]
    vmem = pl.BlockSpec(memory_space=pltpu.VMEM)
    return pl.pallas_call(
        functools.partial(step_kernel, count, peers),
        out_shape=(
            jax.ShapeDtypeStruct((rows, channels), jnp.float32),
            jax.ShapeDtypeStruct((2, rows, b_gain.shape[1]), jnp.float32),
            jax.ShapeDtypeStruct(attn.shape, jnp.bfloat16),
        ),
        in_specs=[vmem] * 7,
        out_specs=(vmem, vmem, vmem),
        scratch_shapes=[
            pltpu.VMEM((count - 1,) + part.shape, jnp.float32),
            pltpu.VMEM((peers - 1,) + attn.shape[1:], jnp.bfloat16),
            pltpu.SemaphoreType.DMA((count - 1,)),
            pltpu.SemaphoreType.DMA((count - 1,)),
            pltpu.SemaphoreType.DMA((peers - 1,)),
            pltpu.SemaphoreType.DMA((peers - 1,)),
        ],
        compiler_params=params(collective_id=0, has_side_effects=True),
        cost_estimate=pl.CostEstimate(
            flops=2 * rows * dt_proj.size, bytes_accessed=2 * dt_proj.size + 4 * rows * channels,
            transcendentals=2 * rows * channels,
        ),
        name="tp_sum_step",
    )(part, attn, dt_proj, dt_bias, dt_gain, b_gain, c_gain)


def update_row(row, prev, dt_ref, signal_ref, bc_ref, decay_ref):
    states = decay_ref.shape[0]
    eye = lax.broadcasted_iota(jnp.int32, (states, states), 0) == lax.broadcasted_iota(
        jnp.int32, (states, states), 1
    )

    def column(which):
        line = bc_ref[which, pl.ds(row, 1), :]
        spread = jnp.where(eye, jnp.broadcast_to(line, (states, states)), 0.0)
        return jnp.sum(spread, axis=1, keepdims=True)

    dt = dt_ref[pl.ds(row, 1), :]
    drive = dt * signal_ref[pl.ds(row, 1), :]
    new = jnp.exp(-dt * decay_ref[...]) * prev + drive * column(0)
    return new, jnp.sum(column(1) * new, axis=0, keepdims=True)


def write_rows(perm, first, news, new_ref, buf_ref, sem):
    step, steps = pl.program_id(0), pl.num_programs(0)

    def copies(at):
        slot = lax.rem(at, 2)
        return [
            pltpu.make_async_copy(
                buf_ref.at[slot, k], new_ref.at[perm[first + at * BATCH + k]], sem.at[slot, k]
            )
            for k in range(BATCH)
        ]

    @pl.when(step >= 2)
    def _():
        for copy in copies(step - 2):
            copy.wait()

    here = copies(step)
    slot = lax.rem(step, 2)
    for k in range(BATCH):
        buf_ref[slot, k] = news(k)
        here[k].start()

    @pl.when(step == steps - 1)
    def _():
        @pl.when(step >= 1)
        def _():
            for copy in copies(step - 1):
                copy.wait()

        for copy in here:
            copy.wait()


def early_kernel(first, perm, *refs):
    states = refs[:BATCH]
    dt_ref, signal_ref, bc_ref, decay_ref, new_ref, y_ref, buf_ref, sem = refs[BATCH:]
    step = pl.program_id(0)

    @pl.when(step == 0)
    def _():
        y_ref[...] = jnp.zeros_like(y_ref)

    def news(k):
        row = perm[first + step * BATCH + k]
        new, y = update_row(row, states[k][0], dt_ref, signal_ref, bc_ref, decay_ref)
        y_ref[pl.ds(row, 1), :] = y
        return new

    write_rows(perm, first, news, new_ref, buf_ref, sem)


def late_kernel(perm, source, *refs):
    states, gots = refs[:BATCH], refs[BATCH : 2 * BATCH]
    (dt_ref, signal_ref, bc_ref, decay_ref, early_y, skip_ref, z_ref, kept_ref, new_ref, out_ref,
     y_ref, buf_ref, sem) = refs[2 * BATCH :]
    step = pl.program_id(0)

    @pl.when(step == 0)
    def _():
        y_ref[...] = early_y[...]

    def news(k):
        row = perm[step * BATCH + k]
        prev = jnp.where(source[row] >= 0, gots[k][0].astype(jnp.float32), states[k][0])
        new, y = update_row(row, prev, dt_ref, signal_ref, bc_ref, decay_ref)
        y_ref[pl.ds(row, 1), :] = y
        return new

    write_rows(perm, 0, news, new_ref, buf_ref, sem)

    @pl.when(step == pl.num_programs(0) - 1)
    def _():
        z = z_ref[...].astype(jnp.float32)
        gate = z / (1.0 + jnp.exp(-z))
        out_ref[...] = ((y_ref[...] + skip_ref[...] * signal_ref[...]) * gate).astype(jnp.bfloat16)


def update_early(perm, state, dt, signal, bc, decay, late):
    rows = state.shape[0]
    block = (1,) + state.shape[1:]
    shared = (dt, signal, bc, decay)

    def spec(k):
        return pl.BlockSpec(block, lambda i, perm: (perm[late + i * BATCH + k], 0, 0))

    return pl.pallas_call(
        functools.partial(early_kernel, late),
        grid_spec=pltpu.PrefetchScalarGridSpec(
            num_scalar_prefetch=1,
            grid=((rows - late) // BATCH,),
            in_specs=[spec(k) for k in range(BATCH)] + [whole(a.shape) for a in shared],
            out_specs=[pl.BlockSpec(memory_space=pl.ANY), whole(dt.shape)],
            scratch_shapes=[
                pltpu.VMEM((2, BATCH) + state.shape[1:], jnp.float32),
                pltpu.SemaphoreType.DMA((2, BATCH)),
            ],
        ),
        out_shape=(
            jax.ShapeDtypeStruct(state.shape, jnp.float32),
            jax.ShapeDtypeStruct(dt.shape, jnp.float32),
        ),
        compiler_params=params(),
        cost_estimate=pl.CostEstimate(
            flops=8 * (rows - late) * state[0].size,
            bytes_accessed=8 * (rows - late) * state[0].size,
            transcendentals=(rows - late) * state[0].size,
        ),
        name="ssm_early",
    )(perm, *([state] * BATCH), *shared)


def update_late(perm, source, state, got, dt, signal, bc, decay, early_y, skip, z, kept, late):
    block = (1,) + state.shape[1:]
    shared = (dt, signal, bc, decay, early_y, skip, z)

    def state_spec(k):
        return pl.BlockSpec(block, lambda i, perm, source: (perm[i * BATCH + k], 0, 0))

    def got_spec(k):
        return pl.BlockSpec(
            block,
            lambda i, perm, source: (jnp.maximum(source[perm[i * BATCH + k]], 0), 0, 0),
        )

    return pl.pallas_call(
        late_kernel,
        grid_spec=pltpu.PrefetchScalarGridSpec(
            num_scalar_prefetch=2,
            grid=(late // BATCH,),
            in_specs=[state_spec(k) for k in range(BATCH)]
            + [got_spec(k) for k in range(BATCH)]
            + [whole(a.shape) for a in shared]
            + [pl.BlockSpec(memory_space=pl.ANY)],
            out_specs=[pl.BlockSpec(memory_space=pl.ANY), whole(dt.shape)],
            scratch_shapes=[
                pltpu.VMEM(dt.shape, jnp.float32),
                pltpu.VMEM((2, BATCH) + state.shape[1:], jnp.float32),
                pltpu.SemaphoreType.DMA((2, BATCH)),
            ],
        ),
        out_shape=(
            jax.ShapeDtypeStruct(state.shape, jnp.float32),
            jax.ShapeDtypeStruct(dt.shape, jnp.bfloat16),
        ),
        input_output_aliases={2 + 2 * BATCH + len(shared): 0},
        compiler_params=params(),
        cost_estimate=pl.CostEstimate(
            flops=8 * late * state[0].size,
            bytes_accessed=10 * late * state[0].size,
            transcendentals=late * state[0].size,
        ),
        name="ssm_late",
    )(perm, source, *([state] * BATCH), *([got] * BATCH), *shared, kept)


def shards(
    x_in,
    z_gate,
    conv_state,
    conv_pool,
    ssm_state,
    ssm_pool,
    conv_weight,
    conv_bias,
    x_proj,
    dt_gain,
    b_gain,
    c_gain,
    dt_proj,
    dt_bias,
    decay_rate,
    skip,
    query,
    new_kv,
    kv_cache,
    kv_pool,
    ctx_len,
    row_owner,
    row_pos,
    swap_slot,
    swap_lens,
    swap_pages,
):
    peer_count = lax.axis_size("rep")
    tp_count = lax.axis_size("tp")
    row_count, channels = x_in.shape
    slot_cap = swap_slot.shape[2]
    entry_count = peer_count * slot_cap
    taps = conv_state.shape[1]
    head_count = query.shape[1] // HD
    slot_list = swap_slot[0].reshape(-1)
    resumed = row_owner >= 0
    source = jnp.where(resumed, row_owner * slot_cap + row_pos, -1).astype(jnp.int32)
    row_ids = jnp.arange(row_count, dtype=jnp.int32)
    before = row_ids[None, :] < row_ids[:, None]
    earlier = jnp.sum((before & (resumed[None, :] == resumed[:, None])).astype(jnp.int32), axis=1)
    place = jnp.where(resumed, earlier, earlier + jnp.sum(resumed.astype(jnp.int32)))
    perm = jnp.sum(
        jnp.where(place[None, :] == row_ids[:, None], row_ids[None, :], 0), axis=1
    ).astype(jnp.int32)

    def exchange(block):
        split = block.reshape((peer_count, slot_cap) + block.shape[1:])
        out = lax.all_to_all(split, "rep", split_axis=0, concat_axis=0, tiled=True)
        return out.reshape(block.shape)

    owner_line, pos_line = row_owner[None, :], row_pos[None, :]
    first = exchange(
        ask(
            slot_cap, owner_line, pos_line, slot_list[None, :], jnp.swapaxes(conv_pool, 0, 1),
            query, new_kv,
        )
    )
    states = pack_states(ssm_pool, slot_list)
    first, states = lax.optimization_barrier((first, states))
    states_in = exchange(states)

    query_rows = query.reshape(row_count, head_count, HD)
    new_rows = new_kv.reshape(row_count, -1, HD)
    attn_here = attend_resident(query_rows, kv_cache, new_rows, ctx_len).reshape(query.shape)

    mixed, new_conv, part = convolve(
        slot_cap, owner_line, pos_line, x_in, jnp.swapaxes(conv_state, 0, 1), first, conv_weight,
        conv_bias[None, :], x_proj.T,
    )
    new_conv = jnp.swapaxes(new_conv, 0, 1)

    query_width = query.shape[1]
    asked = first[:, taps * channels :]
    query_in = asked[:, :query_width].reshape(entry_count, head_count, HD)
    new_in = asked[:, query_width:].reshape(entry_count, -1, HD)
    attn_there = attend_paged(
        query_in, kv_pool, new_in, swap_lens[0].reshape(-1), swap_pages[0].reshape(-1),
        kv_cache.shape[1],
    )
    dt_step, bc, attn_back = step_sizes(
        tp_count, part, attn_there.reshape(peer_count, slot_cap, head_count, HD), dt_proj,
        dt_bias[None, :], dt_gain[None, :], b_gain[None, :], c_gain[None, :],
    )
    attn_back = attn_back.reshape(entry_count, query_width)
    picked = jnp.take(attn_back, jnp.maximum(source, 0), axis=0, mode="clip")
    attn_out = jnp.where(resumed[:, None], picked, attn_here)

    late = min(row_count, entry_count)
    if late < row_count:
        kept, early_y = update_early(perm, ssm_state, dt_step, mixed, bc, decay_rate, late)
    else:
        kept, early_y = jnp.zeros_like(ssm_state), jnp.zeros_like(dt_step)
    new_ssm, mamba_out = update_late(
        perm, source, ssm_state, states_in, dt_step, mixed, bc, decay_rate, early_y,
        skip[None, :], z_gate, kept, late,
    )
    return (mamba_out, attn_out, new_ssm, new_conv)


def solution(mesh):
    in_specs = (
        P("rep", "tp"),
        P("rep", "tp"),
        P("rep", None, "tp"),
        P("rep", None, "tp"),
        P("rep", None, "tp"),
        P("rep", None, "tp"),
        P(None, "tp"),
        P("tp"),
        P("tp", None),
        P(),
        P(),
        P(),
        P(None, "tp"),
        P("tp"),
        P(None, "tp"),
        P("tp"),
        P("rep", "tp"),
        P("rep", "tp"),
        P("rep", None, "tp"),
        P("rep", None, "tp"),
        P("rep"),
        P("rep"),
        P("rep"),
        P("rep", None, None),
        P("rep", None, None),
        P("rep", None, None, None),
    )
    out_specs = (P("rep", "tp"), P("rep", "tp"), P("rep", None, "tp"), P("rep", None, "tp"))
    return jax.shard_map(shards, mesh=mesh, in_specs=in_specs, out_specs=out_specs, check_vma=False)
```

```python
import functools
import math

import jax
import jax.numpy as jnp
from jax import lax
from jax.experimental import pallas as pl
from jax.experimental.pallas import tpu as pltpu
from jax.sharding import PartitionSpec as P

HD = 128
MESH = pl.DeviceIdType.MESH
BATCH = 4
VMEM_LIMIT = 48 * 1024 * 1024


def params(**kw):
    return pltpu.CompilerParams(vmem_limit_bytes=VMEM_LIMIT, **kw)


def whole(shape):
    return pl.BlockSpec(shape, lambda *_: (0,) * len(shape))


def attend_row(q, ctx, nkv, length):
    heads, width = q.shape
    kv_heads = nkv.shape[0] // 2
    groups = heads // kv_heads
    tokens = ctx.shape[0]
    scale = 1.0 / math.sqrt(width)

    def of_head(parts):
        row = lax.broadcasted_iota(jnp.int32, parts[0].shape, 0)
        out = parts[0]
        for k in range(1, kv_heads):
            out = jnp.where(row >= k * groups, parts[k], out)
        return out

    nkv = nkv.astype(jnp.float32)
    q32 = q.astype(jnp.float32)
    scores = of_head(
        [
            lax.dot_general(
                q,
                ctx[:, 2 * k * width : (2 * k + 1) * width],
                (((1,), (1,)), ((), ())),
                preferred_element_type=jnp.float32,
            )
            for k in range(kv_heads)
        ]
    ) * scale
    live = lax.broadcasted_iota(jnp.int32, (heads, tokens), 1) < length
    masked = jnp.where(live, scores, -1e30)
    top = jnp.max(masked, axis=1, keepdims=True)
    prob = jnp.where(live, jnp.exp(masked - top), 0.0).astype(jnp.bfloat16)
    total = jnp.sum(prob.astype(jnp.float32), axis=1, keepdims=True)
    mix = of_head(
        [
            jnp.dot(
                prob,
                ctx[:, (2 * k + 1) * width : (2 * k + 2) * width],
                preferred_element_type=jnp.float32,
            )
            for k in range(kv_heads)
        ]
    )
    new_key = of_head(
        [jnp.broadcast_to(nkv[2 * k : 2 * k + 1], (heads, width)) for k in range(kv_heads)]
    )
    new_value = of_head(
        [jnp.broadcast_to(nkv[2 * k + 1 : 2 * k + 2], (heads, width)) for k in range(kv_heads)]
    )
    new_score = jnp.sum(q32 * new_key, axis=1, keepdims=True) * scale
    peak = jnp.maximum(top, new_score)
    old_scale = jnp.exp(top - peak)
    new_scale = jnp.exp(new_score - peak)
    result = (mix * old_scale + new_scale * new_value) / (total * old_scale + new_scale)
    return result.astype(jnp.bfloat16)


def resident_kernel(lens, q_ref, kv_ref, nkv_ref, out_ref):
    batch = q_ref.shape[0]
    base = pl.program_id(0) * batch
    rows = [attend_row(q_ref[i], kv_ref[i], nkv_ref[i], lens[base + i]) for i in range(batch)]
    for i in range(batch):
        out_ref[i] = rows[i]


def paged_kernel(lens, pages, q_ref, pool_ref, nkv_ref, out_ref, ctx_ref):
    batch = q_ref.shape[0]
    base = pl.program_id(0) * batch
    page = pool_ref.shape[1]
    page_count = ctx_ref.shape[1] // page
    for i in range(batch):
        for j in range(page_count):
            ctx_ref[i, j * page : (j + 1) * page, :] = pool_ref[pages[(base + i) * page_count + j]]
    rows = [attend_row(q_ref[i], ctx_ref[i], nkv_ref[i], lens[base + i]) for i in range(batch)]
    for i in range(batch):
        out_ref[i] = rows[i]


def attend_resident(q, kv, nkv, lens):
    rows, heads, width = q.shape
    tokens, kv_width = kv.shape[1:]
    batch = BATCH
    return pl.pallas_call(
        resident_kernel,
        grid_spec=pltpu.PrefetchScalarGridSpec(
            num_scalar_prefetch=1,
            grid=(rows // batch,),
            in_specs=[
                pl.BlockSpec((batch, heads, width), lambda i, *_: (i, 0, 0)),
                pl.BlockSpec((batch, tokens, kv_width), lambda i, *_: (i, 0, 0)),
                pl.BlockSpec((batch,) + nkv.shape[1:], lambda i, *_: (i, 0, 0)),
            ],
            out_specs=pl.BlockSpec((batch, heads, width), lambda i, *_: (i, 0, 0)),
        ),
        out_shape=jax.ShapeDtypeStruct(q.shape, jnp.bfloat16),
        compiler_params=params(),
        cost_estimate=pl.CostEstimate(
            flops=rows * tokens * heads * width * 8,
            bytes_accessed=2 * kv.size,
            transcendentals=rows * heads * tokens,
        ),
        name="attend_resident",
    )(lens, q, kv, nkv)


def attend_paged(q, pool, nkv, lens, pages, tokens):
    entries, heads, width = q.shape
    batch = BATCH
    return pl.pallas_call(
        paged_kernel,
        grid_spec=pltpu.PrefetchScalarGridSpec(
            num_scalar_prefetch=2,
            grid=(entries // batch,),
            in_specs=[
                pl.BlockSpec((batch, heads, width), lambda i, *_: (i, 0, 0)),
                whole(pool.shape),
                pl.BlockSpec((batch,) + nkv.shape[1:], lambda i, *_: (i, 0, 0)),
            ],
            out_specs=pl.BlockSpec((batch, heads, width), lambda i, *_: (i, 0, 0)),
            scratch_shapes=[pltpu.VMEM((batch, tokens, pool.shape[2]), jnp.bfloat16)],
        ),
        out_shape=jax.ShapeDtypeStruct(q.shape, jnp.bfloat16),
        compiler_params=params(),
        cost_estimate=pl.CostEstimate(
            flops=entries * tokens * heads * width * 8,
            bytes_accessed=2 * pool.size,
            transcendentals=entries * heads * tokens,
        ),
        name="attend_paged",
    )(lens, pages, q, pool, nkv)


def entry_match(owner_ref, pos_ref, entries, cap):
    owner = owner_ref[...]
    source = jnp.where(owner >= 0, owner * cap + pos_ref[...], -1)
    shape = (entries, owner.shape[1])
    hit = lax.broadcasted_iota(jnp.int32, shape, 0) == jnp.broadcast_to(source, shape)
    return jnp.where(hit, 1.0, 0.0).astype(jnp.bfloat16)


def pick(match, rows, contract):
    return lax.dot_general(
        match, rows, (((contract,), (0,)), ((), ())), preferred_element_type=jnp.float32
    )


def greet(partners):
    barrier = pltpu.get_barrier_semaphore()
    for partner in partners:
        pl.semaphore_signal(barrier, inc=1, device_id=partner, device_id_type=MESH)
    return lambda: pl.semaphore_wait(barrier, len(partners))


def trade_kernel(peers, cap, slots_ref, owner_hbm, pos_hbm, line_hbm, pool_hbm, query_hbm, new_hbm,
                 states_hbm, got_ref, packed_ref, owner_ref, pos_ref, line_ref, pool_ref,
                 query_ref, new_ref, states_ref, send_ref, load_sem, own_sem, send_sem, recv_sem):
    group = lax.axis_index("rep")
    others = [lax.rem(group + k, peers) for k in range(1, peers)]
    wait_greetings = greet([{"rep": other} for other in others])
    taps, slots, channels = pool_ref.shape
    entries = peers * cap
    loads = [
        pltpu.make_async_copy(src, dst, load_sem.at[k])
        for k, (src, dst) in enumerate(
            (
                (owner_hbm, owner_ref),
                (pos_hbm, pos_ref),
                (line_hbm, line_ref),
                (pool_hbm, pool_ref),
                (query_hbm, query_ref),
                (new_hbm, new_ref),
                (states_hbm, states_ref),
            )
        )
    ]
    for load in loads:
        load.start()
    for load in loads[:-1]:
        load.wait()

    def put(rows, at):
        for p in range(peers):
            send_ref[p, :, at : at + rows.shape[1]] = rows[p * cap : (p + 1) * cap].astype(
                jnp.bfloat16
            )

    shape = (slots, entries)
    hit = lax.broadcasted_iota(jnp.int32, shape, 0) == jnp.broadcast_to(line_ref[...], shape)
    chosen = jnp.where(hit, 1.0, 0.0).astype(jnp.bfloat16)
    for j in range(taps):
        put(pick(chosen, pool_ref[j], 0), j * channels)
    match = entry_match(owner_ref, pos_ref, entries, cap)
    at = taps * channels
    for ref in (query_ref, new_ref):
        put(pick(match, ref[...], 1), at)
        at += ref.shape[1]

    wait_greetings()
    copies = []
    for k, other in enumerate(others):
        copy = pltpu.make_async_remote_copy(
            src_ref=send_ref.at[other],
            dst_ref=got_ref.at[group],
            send_sem=send_sem.at[k],
            recv_sem=recv_sem.at[k],
            device_id={"rep": other},
            device_id_type=MESH,
        )
        copy.start()
        copies.append(copy)
    own = pltpu.make_async_copy(send_ref.at[group], got_ref.at[group], own_sem)
    own.start()
    loads[-1].wait()

    def pack(e, carry):
        packed_ref[e] = states_ref[slots_ref[e]].astype(jnp.bfloat16)
        return carry

    lax.fori_loop(0, entries, pack, 0)
    own.wait()
    for copy in copies:
        copy.wait()


def trade(peers, cap, slots, owner, pos, pool, query, new_kv, states):
    entries = slots.shape[0]
    width = pool.shape[0] * pool.shape[2] + query.shape[1] + new_kv.shape[1]
    anywhere = pl.BlockSpec(memory_space=pl.ANY)
    operands = (owner, pos, slots[None, :], pool, query, new_kv, states)
    return pl.pallas_call(
        functools.partial(trade_kernel, peers, cap),
        in_specs=[pl.BlockSpec(memory_space=pltpu.SMEM)] + [anywhere] * len(operands),
        out_specs=(anywhere, pl.BlockSpec(memory_space=pltpu.VMEM)),
        out_shape=(
            jax.ShapeDtypeStruct((peers, cap, width), jnp.bfloat16),
            jax.ShapeDtypeStruct((entries,) + states.shape[1:], jnp.bfloat16),
        ),
        scratch_shapes=[pltpu.VMEM(a.shape, a.dtype) for a in operands]
        + [
            pltpu.VMEM((peers, cap, width), jnp.bfloat16),
            pltpu.SemaphoreType.DMA((len(operands),)),
            pltpu.SemaphoreType.DMA,
            pltpu.SemaphoreType.DMA((peers - 1,)),
            pltpu.SemaphoreType.DMA((peers - 1,)),
        ],
        compiler_params=params(collective_id=1, has_side_effects=True),
        cost_estimate=pl.CostEstimate(
            flops=2 * entries * pool.size, bytes_accessed=6 * states.size, transcendentals=0
        ),
        name="trade",
    )(slots, *operands)


def home_kernel(peers, attn_ref, back_ref, home_ref, send_sem, recv_sem):
    group = lax.axis_index("rep")
    homes = [lax.rem(group + k, peers) for k in range(1, peers)]
    greet([{"rep": home} for home in homes])()
    copies = []
    for k, home in enumerate(homes):
        copy = pltpu.make_async_remote_copy(
            src_ref=attn_ref.at[home],
            dst_ref=home_ref.at[k],
            send_sem=send_sem.at[k],
            recv_sem=recv_sem.at[k],
            device_id={"rep": home},
            device_id_type=MESH,
        )
        copy.start()
        copies.append(copy)
    back_ref[group] = attn_ref[group]
    for k, copy in enumerate(copies):
        copy.wait_recv()
        back_ref[lax.rem(group + peers - 1 - k, peers)] = home_ref[k]
    for copy in copies:
        copy.wait_send()


def send_home(attn):
    peers = attn.shape[0]
    vmem = pl.BlockSpec(memory_space=pltpu.VMEM)
    return pl.pallas_call(
        functools.partial(home_kernel, peers),
        out_shape=jax.ShapeDtypeStruct(attn.shape, jnp.bfloat16),
        in_specs=[vmem],
        out_specs=vmem,
        scratch_shapes=[
            pltpu.VMEM((peers - 1,) + attn.shape[1:], jnp.bfloat16),
            pltpu.SemaphoreType.DMA((peers - 1,)),
            pltpu.SemaphoreType.DMA((peers - 1,)),
        ],
        compiler_params=params(collective_id=2, has_side_effects=True),
        cost_estimate=pl.CostEstimate(flops=0, bytes_accessed=4 * attn.size, transcendentals=0),
        name="send_home",
    )(attn)


def conv_kernel(cap, owner_ref, pos_ref, x_ref, state_ref, got_ref, weight_ref, bias_ref,
                proj_ref, mixed_ref, conv_ref, part_ref):
    taps, rows, channels = state_ref.shape
    entries = got_ref.shape[0]
    match = entry_match(owner_ref, pos_ref, entries, cap)
    resumed = pick(match, jnp.ones((entries, 128), jnp.bfloat16), 0)[:, :1] > 0.5
    new = x_ref[...]
    total = new.astype(jnp.float32) * weight_ref[taps : taps + 1, :].astype(jnp.float32)
    for j in range(taps):
        theirs = pick(match, got_ref[:, j * channels : (j + 1) * channels], 0)
        prev = jnp.where(resumed, theirs, state_ref[j].astype(jnp.float32))
        if j > 0:
            conv_ref[j - 1] = prev.astype(jnp.bfloat16)
        total = total + prev * weight_ref[j : j + 1, :].astype(jnp.float32)
    conv_ref[taps - 1] = new
    total = total + bias_ref[...]
    mixed = (total / (1.0 + jnp.exp(-total))).astype(jnp.bfloat16)
    mixed_ref[...] = mixed.astype(jnp.float32)
    part_ref[...] = lax.dot_general(
        mixed, proj_ref[...], (((1,), (1,)), ((), ())), preferred_element_type=jnp.float32
    )


def convolve(cap, owner, pos, x_in, state, got, weight, bias, proj):
    rows, channels = x_in.shape
    outs = (
        jax.ShapeDtypeStruct((rows, channels), jnp.float32),
        jax.ShapeDtypeStruct(state.shape, jnp.bfloat16),
        jax.ShapeDtypeStruct((rows, proj.shape[0]), jnp.float32),
    )
    operands = (owner, pos, x_in, state, got, weight, bias, proj)
    return pl.pallas_call(
        functools.partial(conv_kernel, cap),
        grid=(1,),
        in_specs=[whole(a.shape) for a in operands],
        out_specs=[whole(o.shape) for o in outs],
        out_shape=outs,
        compiler_params=params(),
        cost_estimate=pl.CostEstimate(
            flops=2 * rows * proj.size, bytes_accessed=2 * proj.size + 16 * x_in.size,
            transcendentals=x_in.size,
        ),
        name="conv_proj",
    )(*operands)


def step_kernel(count, part_ref, dt_proj_ref, bias_ref, dt_gain_ref, b_gain_ref, c_gain_ref,
                dt_ref, bc_ref, got_ref, send_sem, recv_sem):
    me = lax.axis_index("tp")
    partners = [{"tp": lax.rem(me + k, count)} for k in range(1, count)]
    greet(partners)()
    copies = []
    for k, partner in enumerate(partners):
        copy = pltpu.make_async_remote_copy(
            src_ref=part_ref,
            dst_ref=got_ref.at[k],
            send_sem=send_sem.at[k],
            recv_sem=recv_sem.at[k],
            device_id=partner,
            device_id_type=MESH,
        )
        copy.start()
        copies.append(copy)
    proj = part_ref[...]
    for k, copy in enumerate(copies):
        copy.wait_recv()
        proj = proj + got_ref[k]
    rank = dt_proj_ref.shape[0]
    states = b_gain_ref.shape[1]

    def rms_scaled(values, gain):
        mean = jnp.mean(values * values, axis=-1, keepdims=True)
        return (values * lax.rsqrt(mean + 1e-06) * gain).astype(jnp.bfloat16)

    normed = rms_scaled(proj[:, :rank], dt_gain_ref[...])
    raw = jnp.dot(normed, dt_proj_ref[...], preferred_element_type=jnp.float32) + bias_ref[...]
    dt_ref[...] = jnp.maximum(raw, 0.0) + jnp.log1p(jnp.exp(-jnp.abs(raw)))
    bc_ref[0] = rms_scaled(proj[:, rank : rank + states], b_gain_ref[...]).astype(jnp.float32)
    bc_ref[1] = rms_scaled(proj[:, rank + states :], c_gain_ref[...]).astype(jnp.float32)
    for copy in copies:
        copy.wait_send()


def step_sizes(count, part, dt_proj, dt_bias, dt_gain, b_gain, c_gain):
    rows = part.shape[0]
    channels = dt_proj.shape[1]
    vmem = pl.BlockSpec(memory_space=pltpu.VMEM)
    return pl.pallas_call(
        functools.partial(step_kernel, count),
        out_shape=(
            jax.ShapeDtypeStruct((rows, channels), jnp.float32),
            jax.ShapeDtypeStruct((2, rows, b_gain.shape[1]), jnp.float32),
        ),
        in_specs=[vmem] * 6,
        out_specs=(vmem, vmem),
        scratch_shapes=[
            pltpu.VMEM((count - 1,) + part.shape, jnp.float32),
            pltpu.SemaphoreType.DMA((count - 1,)),
            pltpu.SemaphoreType.DMA((count - 1,)),
        ],
        compiler_params=params(collective_id=0, has_side_effects=True),
        cost_estimate=pl.CostEstimate(
            flops=2 * rows * dt_proj.size, bytes_accessed=2 * dt_proj.size + 4 * rows * channels,
            transcendentals=2 * rows * channels,
        ),
        name="tp_sum_step",
    )(part, dt_proj, dt_bias, dt_gain, b_gain, c_gain)


def update_row(row, prev, dt_ref, signal_ref, bc_ref, decay_ref):
    states = decay_ref.shape[0]
    eye = lax.broadcasted_iota(jnp.int32, (states, states), 0) == lax.broadcasted_iota(
        jnp.int32, (states, states), 1
    )

    def column(which):
        line = bc_ref[which, pl.ds(row, 1), :]
        spread = jnp.where(eye, jnp.broadcast_to(line, (states, states)), 0.0)
        return jnp.sum(spread, axis=1, keepdims=True)

    dt = dt_ref[pl.ds(row, 1), :]
    drive = dt * signal_ref[pl.ds(row, 1), :]
    new = jnp.exp(-dt * decay_ref[...]) * prev + drive * column(0)
    return new, jnp.sum(column(1) * new, axis=0, keepdims=True)


def write_rows(perm, first, news, new_ref, buf_ref, sem):
    step, steps = pl.program_id(0), pl.num_programs(0)

    def copies(at):
        slot = lax.rem(at, 2)
        return [
            pltpu.make_async_copy(
                buf_ref.at[slot, k], new_ref.at[perm[first + at * BATCH + k]], sem.at[slot, k]
            )
            for k in range(BATCH)
        ]

    @pl.when(step >= 2)
    def _():
        for copy in copies(step - 2):
            copy.wait()

    here = copies(step)
    slot = lax.rem(step, 2)
    for k in range(BATCH):
        buf_ref[slot, k] = news(k)
        here[k].start()

    @pl.when(step == steps - 1)
    def _():
        @pl.when(step >= 1)
        def _():
            for copy in copies(step - 1):
                copy.wait()

        for copy in here:
            copy.wait()


def early_kernel(first, perm, *refs):
    states = refs[:BATCH]
    dt_ref, signal_ref, bc_ref, decay_ref, new_ref, y_ref, buf_ref, sem = refs[BATCH:]
    step = pl.program_id(0)

    @pl.when(step == 0)
    def _():
        y_ref[...] = jnp.zeros_like(y_ref)

    def news(k):
        row = perm[first + step * BATCH + k]
        new, y = update_row(row, states[k][0], dt_ref, signal_ref, bc_ref, decay_ref)
        y_ref[pl.ds(row, 1), :] = y
        return new

    write_rows(perm, first, news, new_ref, buf_ref, sem)


def late_kernel(perm, source, *refs):
    states, gots = refs[:BATCH], refs[BATCH : 2 * BATCH]
    (dt_ref, signal_ref, bc_ref, decay_ref, early_y, skip_ref, z_ref, kept_ref, new_ref, out_ref,
     y_ref, buf_ref, sem) = refs[2 * BATCH :]
    step = pl.program_id(0)

    @pl.when(step == 0)
    def _():
        y_ref[...] = early_y[...]

    def news(k):
        row = perm[step * BATCH + k]
        prev = jnp.where(source[row] >= 0, gots[k][0].astype(jnp.float32), states[k][0])
        new, y = update_row(row, prev, dt_ref, signal_ref, bc_ref, decay_ref)
        y_ref[pl.ds(row, 1), :] = y
        return new

    write_rows(perm, 0, news, new_ref, buf_ref, sem)

    @pl.when(step == pl.num_programs(0) - 1)
    def _():
        z = z_ref[...].astype(jnp.float32)
        gate = z / (1.0 + jnp.exp(-z))
        out_ref[...] = ((y_ref[...] + skip_ref[...] * signal_ref[...]) * gate).astype(jnp.bfloat16)


def update_early(perm, state, dt, signal, bc, decay, late):
    rows = state.shape[0]
    block = (1,) + state.shape[1:]
    shared = (dt, signal, bc, decay)

    def spec(k):
        return pl.BlockSpec(block, lambda i, perm: (perm[late + i * BATCH + k], 0, 0))

    return pl.pallas_call(
        functools.partial(early_kernel, late),
        grid_spec=pltpu.PrefetchScalarGridSpec(
            num_scalar_prefetch=1,
            grid=((rows - late) // BATCH,),
            in_specs=[spec(k) for k in range(BATCH)] + [whole(a.shape) for a in shared],
            out_specs=[pl.BlockSpec(memory_space=pl.ANY), whole(dt.shape)],
            scratch_shapes=[
                pltpu.VMEM((2, BATCH) + state.shape[1:], jnp.float32),
                pltpu.SemaphoreType.DMA((2, BATCH)),
            ],
        ),
        out_shape=(
            jax.ShapeDtypeStruct(state.shape, jnp.float32),
            jax.ShapeDtypeStruct(dt.shape, jnp.float32),
        ),
        compiler_params=params(),
        cost_estimate=pl.CostEstimate(
            flops=8 * (rows - late) * state[0].size,
            bytes_accessed=8 * (rows - late) * state[0].size,
            transcendentals=(rows - late) * state[0].size,
        ),
        name="ssm_early",
    )(perm, *([state] * BATCH), *shared)


def update_late(perm, source, state, got, dt, signal, bc, decay, early_y, skip, z, kept, late):
    block = (1,) + state.shape[1:]
    shared = (dt, signal, bc, decay, early_y, skip, z)

    def state_spec(k):
        return pl.BlockSpec(block, lambda i, perm, source: (perm[i * BATCH + k], 0, 0))

    def got_spec(k):
        return pl.BlockSpec(
            block,
            lambda i, perm, source: (jnp.maximum(source[perm[i * BATCH + k]], 0), 0, 0),
        )

    return pl.pallas_call(
        late_kernel,
        grid_spec=pltpu.PrefetchScalarGridSpec(
            num_scalar_prefetch=2,
            grid=(late // BATCH,),
            in_specs=[state_spec(k) for k in range(BATCH)]
            + [got_spec(k) for k in range(BATCH)]
            + [whole(a.shape) for a in shared]
            + [pl.BlockSpec(memory_space=pl.ANY)],
            out_specs=[pl.BlockSpec(memory_space=pl.ANY), whole(dt.shape)],
            scratch_shapes=[
                pltpu.VMEM(dt.shape, jnp.float32),
                pltpu.VMEM((2, BATCH) + state.shape[1:], jnp.float32),
                pltpu.SemaphoreType.DMA((2, BATCH)),
            ],
        ),
        out_shape=(
            jax.ShapeDtypeStruct(state.shape, jnp.float32),
            jax.ShapeDtypeStruct(dt.shape, jnp.bfloat16),
        ),
        input_output_aliases={2 + 2 * BATCH + len(shared): 0},
        compiler_params=params(),
        cost_estimate=pl.CostEstimate(
            flops=8 * late * state[0].size,
            bytes_accessed=10 * late * state[0].size,
            transcendentals=late * state[0].size,
        ),
        name="ssm_late",
    )(perm, source, *([state] * BATCH), *([got] * BATCH), *shared, kept)


def shards(
    x_in,
    z_gate,
    conv_state,
    conv_pool,
    ssm_state,
    ssm_pool,
    conv_weight,
    conv_bias,
    x_proj,
    dt_gain,
    b_gain,
    c_gain,
    dt_proj,
    dt_bias,
    decay_rate,
    skip,
    query,
    new_kv,
    kv_cache,
    kv_pool,
    ctx_len,
    row_owner,
    row_pos,
    swap_slot,
    swap_lens,
    swap_pages,
):
    peer_count = lax.axis_size("rep")
    tp_count = lax.axis_size("tp")
    row_count, channels = x_in.shape
    slot_cap = swap_slot.shape[2]
    entry_count = peer_count * slot_cap
    taps = conv_state.shape[1]
    head_count = query.shape[1] // HD
    slot_list = swap_slot[0].reshape(-1)
    resumed = row_owner >= 0
    source = jnp.where(resumed, row_owner * slot_cap + row_pos, -1).astype(jnp.int32)
    row_ids = jnp.arange(row_count, dtype=jnp.int32)
    before = row_ids[None, :] < row_ids[:, None]
    earlier = jnp.sum((before & (resumed[None, :] == resumed[:, None])).astype(jnp.int32), axis=1)
    place = jnp.where(resumed, earlier, earlier + jnp.sum(resumed.astype(jnp.int32)))
    perm = jnp.sum(
        jnp.where(place[None, :] == row_ids[:, None], row_ids[None, :], 0), axis=1
    ).astype(jnp.int32)

    owner_line, pos_line = row_owner[None, :], row_pos[None, :]
    first, states = trade(
        peer_count, slot_cap, slot_list, owner_line, pos_line, jnp.swapaxes(conv_pool, 0, 1),
        query, new_kv, ssm_pool,
    )
    first = first.reshape(entry_count, -1)
    states_in = lax.all_to_all(
        states.reshape((peer_count, slot_cap) + states.shape[1:]), "rep", split_axis=0,
        concat_axis=0, tiled=True,
    ).reshape(states.shape)

    query_rows = query.reshape(row_count, head_count, HD)
    new_rows = new_kv.reshape(row_count, -1, HD)
    attn_here = attend_resident(query_rows, kv_cache, new_rows, ctx_len).reshape(query.shape)

    mixed, new_conv, part = convolve(
        slot_cap, owner_line, pos_line, x_in, jnp.swapaxes(conv_state, 0, 1), first, conv_weight,
        conv_bias[None, :], x_proj.T,
    )
    new_conv = jnp.swapaxes(new_conv, 0, 1)

    query_width = query.shape[1]
    asked = first[:, taps * channels :]
    query_in = asked[:, :query_width].reshape(entry_count, head_count, HD)
    new_in = asked[:, query_width:].reshape(entry_count, -1, HD)
    attn_there = attend_paged(
        query_in, kv_pool, new_in, swap_lens[0].reshape(-1), swap_pages[0].reshape(-1),
        kv_cache.shape[1],
    )
    dt_step, bc = step_sizes(
        tp_count, part, dt_proj, dt_bias[None, :], dt_gain[None, :], b_gain[None, :],
        c_gain[None, :],
    )
    late = min(row_count, entry_count)
    if late < row_count:
        kept, early_y = update_early(perm, ssm_state, dt_step, mixed, bc, decay_rate, late)
    else:
        kept, early_y = jnp.zeros_like(ssm_state), jnp.zeros_like(dt_step)
    attn_there, early_y = lax.optimization_barrier((attn_there, early_y))
    attn_back = send_home(attn_there.reshape(peer_count, slot_cap, head_count, HD))
    attn_back, early_y = lax.optimization_barrier((attn_back, early_y))
    attn_back = attn_back.reshape(entry_count, query_width)
    picked = jnp.take(attn_back, jnp.maximum(source, 0), axis=0, mode="clip")
    attn_out = jnp.where(resumed[:, None], picked, attn_here)
    new_ssm, mamba_out = update_late(
        perm, source, ssm_state, states_in, dt_step, mixed, bc, decay_rate, early_y,
        skip[None, :], z_gate, kept, late,
    )
    return (mamba_out, attn_out, new_ssm, new_conv)


def solution(mesh):
    in_specs = (
        P("rep", "tp"),
        P("rep", "tp"),
        P("rep", None, "tp"),
        P("rep", None, "tp"),
        P("rep", None, "tp"),
        P("rep", None, "tp"),
        P(None, "tp"),
        P("tp"),
        P("tp", None),
        P(),
        P(),
        P(),
        P(None, "tp"),
        P("tp"),
        P(None, "tp"),
        P("tp"),
        P("rep", "tp"),
        P("rep", "tp"),
        P("rep", None, "tp"),
        P("rep", None, "tp"),
        P("rep"),
        P("rep"),
        P("rep"),
        P("rep", None, None),
        P("rep", None, None),
        P("rep", None, None, None),
    )
    out_specs = (P("rep", "tp"), P("rep", "tp"), P("rep", None, "tp"), P("rep", None, "tp"))
    return jax.shard_map(shards, mesh=mesh, in_specs=in_specs, out_specs=out_specs, check_vma=False)
```

```python
import functools
import math

import jax
import jax.numpy as jnp
from jax import lax
from jax.experimental import pallas as pl
from jax.experimental.pallas import tpu as pltpu
from jax.sharding import PartitionSpec as P

HD = 128
MESH = pl.DeviceIdType.MESH
BATCH = 4
VMEM_LIMIT = 48 * 1024 * 1024


def params(**kw):
    return pltpu.CompilerParams(vmem_limit_bytes=VMEM_LIMIT, **kw)


def whole(shape):
    return pl.BlockSpec(shape, lambda *_: (0,) * len(shape))


def attend_row(q, ctx, nkv, length):
    heads, width = q.shape
    kv_heads = nkv.shape[0] // 2
    groups = heads // kv_heads
    tokens = ctx.shape[0]
    scale = 1.0 / math.sqrt(width)

    def of_head(parts):
        row = lax.broadcasted_iota(jnp.int32, parts[0].shape, 0)
        out = parts[0]
        for k in range(1, kv_heads):
            out = jnp.where(row >= k * groups, parts[k], out)
        return out

    nkv = nkv.astype(jnp.float32)
    q32 = q.astype(jnp.float32)
    scores = of_head(
        [
            lax.dot_general(
                q,
                ctx[:, 2 * k * width : (2 * k + 1) * width],
                (((1,), (1,)), ((), ())),
                preferred_element_type=jnp.float32,
            )
            for k in range(kv_heads)
        ]
    ) * scale
    live = lax.broadcasted_iota(jnp.int32, (heads, tokens), 1) < length
    masked = jnp.where(live, scores, -1e30)
    top = jnp.max(masked, axis=1, keepdims=True)
    prob = jnp.where(live, jnp.exp(masked - top), 0.0).astype(jnp.bfloat16)
    total = jnp.sum(prob.astype(jnp.float32), axis=1, keepdims=True)
    mix = of_head(
        [
            jnp.dot(
                prob,
                ctx[:, (2 * k + 1) * width : (2 * k + 2) * width],
                preferred_element_type=jnp.float32,
            )
            for k in range(kv_heads)
        ]
    )
    new_key = of_head(
        [jnp.broadcast_to(nkv[2 * k : 2 * k + 1], (heads, width)) for k in range(kv_heads)]
    )
    new_value = of_head(
        [jnp.broadcast_to(nkv[2 * k + 1 : 2 * k + 2], (heads, width)) for k in range(kv_heads)]
    )
    new_score = jnp.sum(q32 * new_key, axis=1, keepdims=True) * scale
    peak = jnp.maximum(top, new_score)
    old_scale = jnp.exp(top - peak)
    new_scale = jnp.exp(new_score - peak)
    result = (mix * old_scale + new_scale * new_value) / (total * old_scale + new_scale)
    return result.astype(jnp.bfloat16)


def resident_kernel(lens, q_ref, kv_ref, nkv_ref, out_ref):
    batch = q_ref.shape[0]
    base = pl.program_id(0) * batch
    rows = [attend_row(q_ref[i], kv_ref[i], nkv_ref[i], lens[base + i]) for i in range(batch)]
    for i in range(batch):
        out_ref[i] = rows[i]


def paged_kernel(lens, pages, q_ref, pool_ref, nkv_ref, out_ref, ctx_ref):
    batch = q_ref.shape[0]
    base = pl.program_id(0) * batch
    page = pool_ref.shape[1]
    page_count = ctx_ref.shape[1] // page
    for i in range(batch):
        for j in range(page_count):
            ctx_ref[i, j * page : (j + 1) * page, :] = pool_ref[pages[(base + i) * page_count + j]]
    rows = [attend_row(q_ref[i], ctx_ref[i], nkv_ref[i], lens[base + i]) for i in range(batch)]
    for i in range(batch):
        out_ref[i] = rows[i]


def attend_resident(q, kv, nkv, lens):
    rows, heads, width = q.shape
    tokens, kv_width = kv.shape[1:]
    batch = BATCH
    return pl.pallas_call(
        resident_kernel,
        grid_spec=pltpu.PrefetchScalarGridSpec(
            num_scalar_prefetch=1,
            grid=(rows // batch,),
            in_specs=[
                pl.BlockSpec((batch, heads, width), lambda i, *_: (i, 0, 0)),
                pl.BlockSpec((batch, tokens, kv_width), lambda i, *_: (i, 0, 0)),
                pl.BlockSpec((batch,) + nkv.shape[1:], lambda i, *_: (i, 0, 0)),
            ],
            out_specs=pl.BlockSpec((batch, heads, width), lambda i, *_: (i, 0, 0)),
        ),
        out_shape=jax.ShapeDtypeStruct(q.shape, jnp.bfloat16),
        compiler_params=params(),
        cost_estimate=pl.CostEstimate(
            flops=rows * tokens * heads * width * 8,
            bytes_accessed=2 * kv.size,
            transcendentals=rows * heads * tokens,
        ),
        name="attend_resident",
    )(lens, q, kv, nkv)


def attend_paged(q, pool, nkv, lens, pages, tokens):
    entries, heads, width = q.shape
    batch = BATCH
    return pl.pallas_call(
        paged_kernel,
        grid_spec=pltpu.PrefetchScalarGridSpec(
            num_scalar_prefetch=2,
            grid=(entries // batch,),
            in_specs=[
                pl.BlockSpec((batch, heads, width), lambda i, *_: (i, 0, 0)),
                whole(pool.shape),
                pl.BlockSpec((batch,) + nkv.shape[1:], lambda i, *_: (i, 0, 0)),
            ],
            out_specs=pl.BlockSpec((batch, heads, width), lambda i, *_: (i, 0, 0)),
            scratch_shapes=[pltpu.VMEM((batch, tokens, pool.shape[2]), jnp.bfloat16)],
        ),
        out_shape=jax.ShapeDtypeStruct(q.shape, jnp.bfloat16),
        compiler_params=params(),
        cost_estimate=pl.CostEstimate(
            flops=entries * tokens * heads * width * 8,
            bytes_accessed=2 * pool.size,
            transcendentals=entries * heads * tokens,
        ),
        name="attend_paged",
    )(lens, pages, q, pool, nkv)


def entry_match(owner_ref, pos_ref, entries, cap):
    owner = owner_ref[...]
    source = jnp.where(owner >= 0, owner * cap + pos_ref[...], -1)
    shape = (entries, owner.shape[1])
    hit = lax.broadcasted_iota(jnp.int32, shape, 0) == jnp.broadcast_to(source, shape)
    return jnp.where(hit, 1.0, 0.0).astype(jnp.bfloat16)


def pick(match, rows, contract):
    return lax.dot_general(
        match, rows, (((contract,), (0,)), ((), ())), preferred_element_type=jnp.float32
    )


def greet(partners):
    barrier = pltpu.get_barrier_semaphore()
    for partner in partners:
        pl.semaphore_signal(barrier, inc=1, device_id=partner, device_id_type=MESH)
    return lambda: pl.semaphore_wait(barrier, len(partners))


def trade_kernel(peers, cap, slots_ref, owner_hbm, pos_hbm, line_hbm, pool_hbm, query_hbm, new_hbm,
                 states_hbm, got_ref, packed_ref, owner_ref, pos_ref, line_ref, pool_ref,
                 query_ref, new_ref, states_ref, send_ref, pack_ref, load_sem, own_sem, send_sem,
                 recv_sem):
    group = lax.axis_index("rep")
    others = [lax.rem(group + k, peers) for k in range(1, peers)]
    wait_greetings = greet([{"rep": other} for other in others])
    taps, slots, channels = pool_ref.shape
    entries = peers * cap
    loads = [
        pltpu.make_async_copy(src, dst, load_sem.at[k])
        for k, (src, dst) in enumerate(
            (
                (owner_hbm, owner_ref),
                (pos_hbm, pos_ref),
                (line_hbm, line_ref),
                (pool_hbm, pool_ref),
                (query_hbm, query_ref),
                (new_hbm, new_ref),
                (states_hbm, states_ref),
            )
        )
    ]
    for load in loads:
        load.start()
    for load in loads[:-1]:
        load.wait()

    def put(rows, at):
        for p in range(peers):
            send_ref[p, :, at : at + rows.shape[1]] = rows[p * cap : (p + 1) * cap].astype(
                jnp.bfloat16
            )

    shape = (slots, entries)
    hit = lax.broadcasted_iota(jnp.int32, shape, 0) == jnp.broadcast_to(line_ref[...], shape)
    chosen = jnp.where(hit, 1.0, 0.0).astype(jnp.bfloat16)
    for j in range(taps):
        put(pick(chosen, pool_ref[j], 0), j * channels)
    match = entry_match(owner_ref, pos_ref, entries, cap)
    at = taps * channels
    for ref in (query_ref, new_ref):
        put(pick(match, ref[...], 1), at)
        at += ref.shape[1]

    wait_greetings()
    copies = []
    for k, other in enumerate(others):
        copy = pltpu.make_async_remote_copy(
            src_ref=send_ref.at[other],
            dst_ref=got_ref.at[group],
            send_sem=send_sem.at[k],
            recv_sem=recv_sem.at[k],
            device_id={"rep": other},
            device_id_type=MESH,
        )
        copy.start()
        copies.append(copy)
    own = pltpu.make_async_copy(send_ref.at[group], got_ref.at[group], own_sem)
    own.start()
    loads[-1].wait()

    def pack(e, carry):
        pack_ref[e] = states_ref[slots_ref[e]].astype(jnp.bfloat16)
        return carry

    lax.fori_loop(0, entries, pack, 0)
    packed = pltpu.make_async_copy(pack_ref, packed_ref, load_sem.at[len(loads)])
    packed.start()
    packed.wait()
    own.wait()
    for copy in copies:
        copy.wait()


def trade(peers, cap, slots, owner, pos, pool, query, new_kv, states):
    entries = slots.shape[0]
    width = pool.shape[0] * pool.shape[2] + query.shape[1] + new_kv.shape[1]
    anywhere = pl.BlockSpec(memory_space=pl.ANY)
    operands = (owner, pos, slots[None, :], pool, query, new_kv, states)
    return pl.pallas_call(
        functools.partial(trade_kernel, peers, cap),
        in_specs=[pl.BlockSpec(memory_space=pltpu.SMEM)] + [anywhere] * len(operands),
        out_specs=(anywhere, anywhere),
        out_shape=(
            jax.ShapeDtypeStruct((peers, cap, width), jnp.bfloat16),
            jax.ShapeDtypeStruct((entries,) + states.shape[1:], jnp.bfloat16),
        ),
        scratch_shapes=[pltpu.VMEM(a.shape, a.dtype) for a in operands]
        + [
            pltpu.VMEM((peers, cap, width), jnp.bfloat16),
            pltpu.VMEM((entries,) + states.shape[1:], jnp.bfloat16),
            pltpu.SemaphoreType.DMA((len(operands) + 1,)),
            pltpu.SemaphoreType.DMA,
            pltpu.SemaphoreType.DMA((peers - 1,)),
            pltpu.SemaphoreType.DMA((peers - 1,)),
        ],
        compiler_params=pltpu.CompilerParams(collective_id=1, has_side_effects=True),
        cost_estimate=pl.CostEstimate(
            flops=2 * entries * pool.size, bytes_accessed=6 * states.size, transcendentals=0
        ),
        name="trade",
    )(slots, *operands)


def home_kernel(peers, attn_ref, back_ref, home_ref, send_sem, recv_sem):
    group = lax.axis_index("rep")
    homes = [lax.rem(group + k, peers) for k in range(1, peers)]
    greet([{"rep": home} for home in homes])()
    copies = []
    for k, home in enumerate(homes):
        copy = pltpu.make_async_remote_copy(
            src_ref=attn_ref.at[home],
            dst_ref=home_ref.at[k],
            send_sem=send_sem.at[k],
            recv_sem=recv_sem.at[k],
            device_id={"rep": home},
            device_id_type=MESH,
        )
        copy.start()
        copies.append(copy)
    back_ref[group] = attn_ref[group]
    for k, copy in enumerate(copies):
        copy.wait_recv()
        back_ref[lax.rem(group + peers - 1 - k, peers)] = home_ref[k]
    for copy in copies:
        copy.wait_send()


def send_home(attn):
    peers = attn.shape[0]
    vmem = pl.BlockSpec(memory_space=pltpu.VMEM)
    return pl.pallas_call(
        functools.partial(home_kernel, peers),
        out_shape=jax.ShapeDtypeStruct(attn.shape, jnp.bfloat16),
        in_specs=[vmem],
        out_specs=vmem,
        scratch_shapes=[
            pltpu.VMEM((peers - 1,) + attn.shape[1:], jnp.bfloat16),
            pltpu.SemaphoreType.DMA((peers - 1,)),
            pltpu.SemaphoreType.DMA((peers - 1,)),
        ],
        compiler_params=params(collective_id=2, has_side_effects=True),
        cost_estimate=pl.CostEstimate(flops=0, bytes_accessed=4 * attn.size, transcendentals=0),
        name="send_home",
    )(attn)


def conv_kernel(cap, owner_ref, pos_ref, x_ref, state_ref, got_ref, weight_ref, bias_ref,
                proj_ref, mixed_ref, conv_ref, part_ref):
    taps, rows, channels = state_ref.shape
    entries = got_ref.shape[0]
    match = entry_match(owner_ref, pos_ref, entries, cap)
    resumed = pick(match, jnp.ones((entries, 128), jnp.bfloat16), 0)[:, :1] > 0.5
    new = x_ref[...]
    total = new.astype(jnp.float32) * weight_ref[taps : taps + 1, :].astype(jnp.float32)
    for j in range(taps):
        theirs = pick(match, got_ref[:, j * channels : (j + 1) * channels], 0)
        prev = jnp.where(resumed, theirs, state_ref[j].astype(jnp.float32))
        if j > 0:
            conv_ref[j - 1] = prev.astype(jnp.bfloat16)
        total = total + prev * weight_ref[j : j + 1, :].astype(jnp.float32)
    conv_ref[taps - 1] = new
    total = total + bias_ref[...]
    mixed = (total / (1.0 + jnp.exp(-total))).astype(jnp.bfloat16)
    mixed_ref[...] = mixed.astype(jnp.float32)
    part_ref[...] = lax.dot_general(
        mixed, proj_ref[...], (((1,), (1,)), ((), ())), preferred_element_type=jnp.float32
    )


def convolve(cap, owner, pos, x_in, state, got, weight, bias, proj):
    rows, channels = x_in.shape
    outs = (
        jax.ShapeDtypeStruct((rows, channels), jnp.float32),
        jax.ShapeDtypeStruct(state.shape, jnp.bfloat16),
        jax.ShapeDtypeStruct((rows, proj.shape[0]), jnp.float32),
    )
    operands = (owner, pos, x_in, state, got, weight, bias, proj)
    return pl.pallas_call(
        functools.partial(conv_kernel, cap),
        grid=(1,),
        in_specs=[whole(a.shape) for a in operands],
        out_specs=[whole(o.shape) for o in outs],
        out_shape=outs,
        compiler_params=params(),
        cost_estimate=pl.CostEstimate(
            flops=2 * rows * proj.size, bytes_accessed=2 * proj.size + 16 * x_in.size,
            transcendentals=x_in.size,
        ),
        name="conv_proj",
    )(*operands)


def step_kernel(count, part_ref, dt_proj_ref, bias_ref, dt_gain_ref, b_gain_ref, c_gain_ref,
                dt_ref, bc_ref, got_ref, send_sem, recv_sem):
    me = lax.axis_index("tp")
    partners = [{"tp": lax.rem(me + k, count)} for k in range(1, count)]
    greet(partners)()
    copies = []
    for k, partner in enumerate(partners):
        copy = pltpu.make_async_remote_copy(
            src_ref=part_ref,
            dst_ref=got_ref.at[k],
            send_sem=send_sem.at[k],
            recv_sem=recv_sem.at[k],
            device_id=partner,
            device_id_type=MESH,
        )
        copy.start()
        copies.append(copy)
    proj = part_ref[...]
    for k, copy in enumerate(copies):
        copy.wait_recv()
        proj = proj + got_ref[k]
    rank = dt_proj_ref.shape[0]
    states = b_gain_ref.shape[1]

    def rms_scaled(values, gain):
        mean = jnp.mean(values * values, axis=-1, keepdims=True)
        return (values * lax.rsqrt(mean + 1e-06) * gain).astype(jnp.bfloat16)

    normed = rms_scaled(proj[:, :rank], dt_gain_ref[...])
    raw = jnp.dot(normed, dt_proj_ref[...], preferred_element_type=jnp.float32) + bias_ref[...]
    dt_ref[...] = jnp.maximum(raw, 0.0) + jnp.log1p(jnp.exp(-jnp.abs(raw)))
    bc_ref[0] = rms_scaled(proj[:, rank : rank + states], b_gain_ref[...]).astype(jnp.float32)
    bc_ref[1] = rms_scaled(proj[:, rank + states :], c_gain_ref[...]).astype(jnp.float32)
    for copy in copies:
        copy.wait_send()


def step_sizes(count, part, dt_proj, dt_bias, dt_gain, b_gain, c_gain):
    rows = part.shape[0]
    channels = dt_proj.shape[1]
    vmem = pl.BlockSpec(memory_space=pltpu.VMEM)
    return pl.pallas_call(
        functools.partial(step_kernel, count),
        out_shape=(
            jax.ShapeDtypeStruct((rows, channels), jnp.float32),
            jax.ShapeDtypeStruct((2, rows, b_gain.shape[1]), jnp.float32),
        ),
        in_specs=[vmem] * 6,
        out_specs=(vmem, vmem),
        scratch_shapes=[
            pltpu.VMEM((count - 1,) + part.shape, jnp.float32),
            pltpu.SemaphoreType.DMA((count - 1,)),
            pltpu.SemaphoreType.DMA((count - 1,)),
        ],
        compiler_params=params(collective_id=0, has_side_effects=True),
        cost_estimate=pl.CostEstimate(
            flops=2 * rows * dt_proj.size, bytes_accessed=2 * dt_proj.size + 4 * rows * channels,
            transcendentals=2 * rows * channels,
        ),
        name="tp_sum_step",
    )(part, dt_proj, dt_bias, dt_gain, b_gain, c_gain)


def update_row(row, prev, dt_ref, signal_ref, bc_ref, decay_ref):
    states = decay_ref.shape[0]
    eye = lax.broadcasted_iota(jnp.int32, (states, states), 0) == lax.broadcasted_iota(
        jnp.int32, (states, states), 1
    )

    def column(which):
        line = bc_ref[which, pl.ds(row, 1), :]
        spread = jnp.where(eye, jnp.broadcast_to(line, (states, states)), 0.0)
        return jnp.sum(spread, axis=1, keepdims=True)

    dt = dt_ref[pl.ds(row, 1), :]
    drive = dt * signal_ref[pl.ds(row, 1), :]
    new = jnp.exp(-dt * decay_ref[...]) * prev + drive * column(0)
    return new, jnp.sum(column(1) * new, axis=0, keepdims=True)


def write_rows(perm, first, news, new_ref, buf_ref, sem):
    step, steps = pl.program_id(0), pl.num_programs(0)

    def copies(at):
        slot = lax.rem(at, 2)
        return [
            pltpu.make_async_copy(
                buf_ref.at[slot, k], new_ref.at[perm[first + at * BATCH + k]], sem.at[slot, k]
            )
            for k in range(BATCH)
        ]

    @pl.when(step >= 2)
    def _():
        for copy in copies(step - 2):
            copy.wait()

    here = copies(step)
    slot = lax.rem(step, 2)
    for k in range(BATCH):
        buf_ref[slot, k] = news(k)
        here[k].start()

    @pl.when(step == steps - 1)
    def _():
        @pl.when(step >= 1)
        def _():
            for copy in copies(step - 1):
                copy.wait()

        for copy in here:
            copy.wait()


def early_kernel(first, perm, *refs):
    states = refs[:BATCH]
    dt_ref, signal_ref, bc_ref, decay_ref, new_ref, y_ref, buf_ref, sem = refs[BATCH:]
    step = pl.program_id(0)

    @pl.when(step == 0)
    def _():
        y_ref[...] = jnp.zeros_like(y_ref)

    def news(k):
        row = perm[first + step * BATCH + k]
        new, y = update_row(row, states[k][0], dt_ref, signal_ref, bc_ref, decay_ref)
        y_ref[pl.ds(row, 1), :] = y
        return new

    write_rows(perm, first, news, new_ref, buf_ref, sem)


def late_kernel(perm, source, *refs):
    states, gots = refs[:BATCH], refs[BATCH : 2 * BATCH]
    (dt_ref, signal_ref, bc_ref, decay_ref, early_y, skip_ref, z_ref, kept_ref, new_ref, out_ref,
     y_ref, buf_ref, sem) = refs[2 * BATCH :]
    step = pl.program_id(0)

    @pl.when(step == 0)
    def _():
        y_ref[...] = early_y[...]

    def news(k):
        row = perm[step * BATCH + k]
        prev = jnp.where(source[row] >= 0, gots[k][0].astype(jnp.float32), states[k][0])
        new, y = update_row(row, prev, dt_ref, signal_ref, bc_ref, decay_ref)
        y_ref[pl.ds(row, 1), :] = y
        return new

    write_rows(perm, 0, news, new_ref, buf_ref, sem)

    @pl.when(step == pl.num_programs(0) - 1)
    def _():
        z = z_ref[...].astype(jnp.float32)
        gate = z / (1.0 + jnp.exp(-z))
        out_ref[...] = ((y_ref[...] + skip_ref[...] * signal_ref[...]) * gate).astype(jnp.bfloat16)


def update_early(perm, state, dt, signal, bc, decay, late):
    rows = state.shape[0]
    block = (1,) + state.shape[1:]
    shared = (dt, signal, bc, decay)

    def spec(k):
        return pl.BlockSpec(block, lambda i, perm: (perm[late + i * BATCH + k], 0, 0))

    return pl.pallas_call(
        functools.partial(early_kernel, late),
        grid_spec=pltpu.PrefetchScalarGridSpec(
            num_scalar_prefetch=1,
            grid=((rows - late) // BATCH,),
            in_specs=[spec(k) for k in range(BATCH)] + [whole(a.shape) for a in shared],
            out_specs=[pl.BlockSpec(memory_space=pl.ANY), whole(dt.shape)],
            scratch_shapes=[
                pltpu.VMEM((2, BATCH) + state.shape[1:], jnp.float32),
                pltpu.SemaphoreType.DMA((2, BATCH)),
            ],
        ),
        out_shape=(
            jax.ShapeDtypeStruct(state.shape, jnp.float32),
            jax.ShapeDtypeStruct(dt.shape, jnp.float32),
        ),
        compiler_params=params(),
        cost_estimate=pl.CostEstimate(
            flops=8 * (rows - late) * state[0].size,
            bytes_accessed=8 * (rows - late) * state[0].size,
            transcendentals=(rows - late) * state[0].size,
        ),
        name="ssm_early",
    )(perm, *([state] * BATCH), *shared)


def update_late(perm, source, state, got, dt, signal, bc, decay, early_y, skip, z, kept, late):
    block = (1,) + state.shape[1:]
    shared = (dt, signal, bc, decay, early_y, skip, z)

    def state_spec(k):
        return pl.BlockSpec(block, lambda i, perm, source: (perm[i * BATCH + k], 0, 0))

    def got_spec(k):
        return pl.BlockSpec(
            block,
            lambda i, perm, source: (jnp.maximum(source[perm[i * BATCH + k]], 0), 0, 0),
        )

    return pl.pallas_call(
        late_kernel,
        grid_spec=pltpu.PrefetchScalarGridSpec(
            num_scalar_prefetch=2,
            grid=(late // BATCH,),
            in_specs=[state_spec(k) for k in range(BATCH)]
            + [got_spec(k) for k in range(BATCH)]
            + [whole(a.shape) for a in shared]
            + [pl.BlockSpec(memory_space=pl.ANY)],
            out_specs=[pl.BlockSpec(memory_space=pl.ANY), whole(dt.shape)],
            scratch_shapes=[
                pltpu.VMEM(dt.shape, jnp.float32),
                pltpu.VMEM((2, BATCH) + state.shape[1:], jnp.float32),
                pltpu.SemaphoreType.DMA((2, BATCH)),
            ],
        ),
        out_shape=(
            jax.ShapeDtypeStruct(state.shape, jnp.float32),
            jax.ShapeDtypeStruct(dt.shape, jnp.bfloat16),
        ),
        input_output_aliases={2 + 2 * BATCH + len(shared): 0},
        compiler_params=pltpu.CompilerParams(),
        cost_estimate=pl.CostEstimate(
            flops=8 * late * state[0].size,
            bytes_accessed=10 * late * state[0].size,
            transcendentals=late * state[0].size,
        ),
        name="ssm_late",
    )(perm, source, *([state] * BATCH), *([got] * BATCH), *shared, kept)


def shards(
    x_in,
    z_gate,
    conv_state,
    conv_pool,
    ssm_state,
    ssm_pool,
    conv_weight,
    conv_bias,
    x_proj,
    dt_gain,
    b_gain,
    c_gain,
    dt_proj,
    dt_bias,
    decay_rate,
    skip,
    query,
    new_kv,
    kv_cache,
    kv_pool,
    ctx_len,
    row_owner,
    row_pos,
    swap_slot,
    swap_lens,
    swap_pages,
):
    peer_count = lax.axis_size("rep")
    tp_count = lax.axis_size("tp")
    row_count, channels = x_in.shape
    slot_cap = swap_slot.shape[2]
    entry_count = peer_count * slot_cap
    taps = conv_state.shape[1]
    head_count = query.shape[1] // HD
    slot_list = swap_slot[0].reshape(-1)
    resumed = row_owner >= 0
    source = jnp.where(resumed, row_owner * slot_cap + row_pos, -1).astype(jnp.int32)
    row_ids = jnp.arange(row_count, dtype=jnp.int32)
    before = row_ids[None, :] < row_ids[:, None]
    earlier = jnp.sum((before & (resumed[None, :] == resumed[:, None])).astype(jnp.int32), axis=1)
    place = jnp.where(resumed, earlier, earlier + jnp.sum(resumed.astype(jnp.int32)))
    perm = jnp.sum(
        jnp.where(place[None, :] == row_ids[:, None], row_ids[None, :], 0), axis=1
    ).astype(jnp.int32)

    owner_line, pos_line = row_owner[None, :], row_pos[None, :]
    first, states = trade(
        peer_count, slot_cap, slot_list, owner_line, pos_line, jnp.swapaxes(conv_pool, 0, 1),
        query, new_kv, ssm_pool,
    )
    first = first.reshape(entry_count, -1)
    states_in = lax.all_to_all(
        states.reshape((peer_count, slot_cap) + states.shape[1:]), "rep", split_axis=0,
        concat_axis=0, tiled=True,
    ).reshape(states.shape)

    query_rows = query.reshape(row_count, head_count, HD)
    new_rows = new_kv.reshape(row_count, -1, HD)
    attn_here = attend_resident(query_rows, kv_cache, new_rows, ctx_len).reshape(query.shape)

    mixed, new_conv, part = convolve(
        slot_cap, owner_line, pos_line, x_in, jnp.swapaxes(conv_state, 0, 1), first, conv_weight,
        conv_bias[None, :], x_proj.T,
    )
    new_conv = jnp.swapaxes(new_conv, 0, 1)

    query_width = query.shape[1]
    asked = first[:, taps * channels :]
    query_in = asked[:, :query_width].reshape(entry_count, head_count, HD)
    new_in = asked[:, query_width:].reshape(entry_count, -1, HD)
    attn_there = attend_paged(
        query_in, kv_pool, new_in, swap_lens[0].reshape(-1), swap_pages[0].reshape(-1),
        kv_cache.shape[1],
    )
    dt_step, bc = step_sizes(
        tp_count, part, dt_proj, dt_bias[None, :], dt_gain[None, :], b_gain[None, :],
        c_gain[None, :],
    )
    late = min(row_count, entry_count)
    if late < row_count:
        kept, early_y = update_early(perm, ssm_state, dt_step, mixed, bc, decay_rate, late)
    else:
        kept, early_y = jnp.zeros_like(ssm_state), jnp.zeros_like(dt_step)
    attn_there, attn_here, early_y = lax.optimization_barrier((attn_there, attn_here, early_y))
    attn_back = send_home(attn_there.reshape(peer_count, slot_cap, head_count, HD))
    attn_back, early_y = lax.optimization_barrier((attn_back, early_y))
    attn_back = attn_back.reshape(entry_count, query_width)
    picked = jnp.take(attn_back, jnp.maximum(source, 0), axis=0, mode="clip")
    attn_out = jnp.where(resumed[:, None], picked, attn_here)
    new_ssm, mamba_out = update_late(
        perm, source, ssm_state, states_in, dt_step, mixed, bc, decay_rate, early_y,
        skip[None, :], z_gate, kept, late,
    )
    return (mamba_out, attn_out, new_ssm, new_conv)


def solution(mesh):
    in_specs = (
        P("rep", "tp"),
        P("rep", "tp"),
        P("rep", None, "tp"),
        P("rep", None, "tp"),
        P("rep", None, "tp"),
        P("rep", None, "tp"),
        P(None, "tp"),
        P("tp"),
        P("tp", None),
        P(),
        P(),
        P(),
        P(None, "tp"),
        P("tp"),
        P(None, "tp"),
        P("tp"),
        P("rep", "tp"),
        P("rep", "tp"),
        P("rep", None, "tp"),
        P("rep", None, "tp"),
        P("rep"),
        P("rep"),
        P("rep"),
        P("rep", None, None),
        P("rep", None, None),
        P("rep", None, None, None),
    )
    out_specs = (P("rep", "tp"), P("rep", "tp"), P("rep", None, "tp"), P("rep", None, "tp"))
    return jax.shard_map(shards, mesh=mesh, in_specs=in_specs, out_specs=out_specs, check_vma=False)
```
